256 devices in a mesh: seq: 8 (over x, core), fsdp: 32 (over y, z).
Axes of the slice: x: 4, y: 4, z: 8, core: 2. Of those that a mesh axis runs over, the one named last changes fastest.
Arguments:
- queries: bfloat16 [32, 1024, 3072], P('fsdp', 'seq'), may hold values from -6 to 6
- attn_keys: bfloat16 [32, 1024, 3072], P('fsdp', 'seq'), may hold values from -6 to 6
- attn_values: bfloat16 [32, 1024, 3072], P('fsdp', 'seq'), may hold values from -6 to 6
- grad_out: bfloat16 [32, 1024, 6144], P('fsdp', 'seq'), may hold values from -6 to 6
- out_weight: bfloat16 [3072, 6144], P('seq', 'fsdp'), may hold values from -0.109375 to 0.109375
Outputs:
- grad_queries: bfloat16 [32, 1024, 3072], P('fsdp', 'seq')
- grad_keys: bfloat16 [32, 1024, 3072], P('fsdp', 'seq')
- grad_values: bfloat16 [32, 1024, 3072], P('fsdp', 'seq')
- grad_weight: float32 [3072, 6144], P('seq', 'fsdp')
The draws below stay inside these ranges and needn't reach their ends.
All inputs are finite; a program needn't handle non-finite values.
Results may differ from the reference program's by a relative error of at most 0.013.
Values may be sent and summed in bfloat16 or wider, within the bound.
No kernel may reach another device: no remote copies, remote signals or barrier semaphores. Data moves between devices by JAX's collectives and lax.ppermute only.
A program may use at most 128 MiB of HBM per device.

```python
import jax
import jax.numpy as jnp
from jax import lax

D = 6144
HEADS = 24
HEAD_DIM = 128
HQ = 3072
LEN = 1024
SEQS = 32


def draw_queries(key, part):
    key = jax.random.fold_in(key, 31)
    base = jax.random.truncated_normal(key, -4.0, 4.0, (SEQS, LEN, HQ), jnp.float32)
    return base.astype(jnp.bfloat16)


def draw_attn_keys(key, part):
    key = jax.random.fold_in(key, 47)
    base = jax.random.truncated_normal(key, -4.0, 4.0, (SEQS, LEN, HQ), jnp.float32)
    return base.astype(jnp.bfloat16)


def strengthened(values, stream_key, source, target, parts, factor):
    owner, partner = [(jnp.arange(values.shape[dim]) // (values.shape[dim] // parts)).reshape([-1 if axis == dim else 1 for axis in range(values.ndim)]) for dim in (source, target)]
    chosen = jax.random.permutation(stream_key, parts)[partner]
    strong = (owner == chosen) | (owner == (partner + parts // 2) % parts)
    return jnp.where(strong, factor * values, values)


def shard_levels(rng, shape, split, low, top_value):
    def one(axis_at, blocks):
        draws = jax.random.uniform(jax.random.fold_in(jax.random.fold_in(rng, 6), axis_at), (blocks,), jnp.float32, low / len(split), top_value / len(split))
        return jnp.repeat(jnp.exp(draws), shape[axis_at] // blocks).reshape((-1,) + (1,) * (len(shape) - axis_at - 1))

    loudness = one(*split[0])
    for cut in split[1:]:
        loudness = loudness * one(*cut)
    return loudness


def normal_values(own_key, dims, deviation, reach, split=(), kind=jnp.bfloat16):
    values = deviation * jax.random.normal(own_key, dims, jnp.float32)
    if split:
        values = values * shard_levels(own_key, dims, split, -0.22, 0.18)
    return jnp.clip(values, -reach, reach).astype(kind)


def bell_draw_with(rng, shape, spread, reach, cuts, heavy, dtype=jnp.bfloat16):
    values = spread * jax.random.normal(rng, shape, jnp.float32)
    if cuts:
        values = values * shard_levels(rng, shape, cuts, -0.22, 0.18)
    return jnp.clip(strengthened(values, jax.random.fold_in(rng, 3), *heavy), -reach, reach).astype(dtype)


def setup_inputs(seed: int = 0) -> dict:
    key_list = jax.random.split(jax.random.key(seed), 6)
    queries = draw_queries(jax.random.fold_in(key_list[5], 71), 0)
    attn_keys = draw_attn_keys(jax.random.fold_in(key_list[5], 71), 0)
    attn_values = normal_values(key_list[2], (SEQS, LEN, HQ), 1.0, 6.0, ((0, 32), (1, 8)))
    grad_out = bell_draw_with(key_list[3], (SEQS, LEN, D), 1.0, 6.0, ((0, 32), (1, 8)), (0, 2, 32, 2.75))
    out_weight = normal_values(key_list[4], (HQ, D), HQ ** -0.5, 0.109375, ((0, 8), (1, 32)))
    return {"queries": queries, "attn_keys": attn_keys, "attn_values": attn_values, "grad_out": grad_out, "out_weight": out_weight}


def head_pass(items):
    q, k, v, dout = items
    scale = 1.0 / (HEAD_DIM ** 0.5)
    scores = jnp.dot(q, k.T, preferred_element_type=jnp.float32) * scale
    top = jnp.max(scores, axis=1, keepdims=True)
    expo = jnp.exp(scores - top)
    probs = expo / jnp.sum(expo, axis=1, keepdims=True)
    probs_low = probs.astype(jnp.bfloat16)
    attended = jnp.dot(probs_low, v, preferred_element_type=jnp.float32).astype(jnp.bfloat16)
    grad_v = jnp.dot(probs_low.T, dout, preferred_element_type=jnp.float32).astype(jnp.bfloat16)
    grad_probs = jnp.dot(dout, v.T, preferred_element_type=jnp.float32)
    delta = jnp.sum(dout.astype(jnp.float32) * attended.astype(jnp.float32), axis=1, keepdims=True)
    grad_scores = (probs * (grad_probs - delta)).astype(jnp.bfloat16)
    grad_q = (jnp.dot(grad_scores, k, preferred_element_type=jnp.float32) * scale).astype(jnp.bfloat16)
    grad_k = (jnp.dot(grad_scores.T, q, preferred_element_type=jnp.float32) * scale).astype(jnp.bfloat16)
    return attended, grad_q, grad_k, grad_v


def split_heads(array):
    return array.reshape(SEQS, LEN, HEADS, HEAD_DIM).transpose(0, 2, 1, 3).reshape(SEQS * HEADS, LEN, HEAD_DIM)


def join_heads(array):
    return array.reshape(SEQS, HEADS, LEN, HEAD_DIM).transpose(0, 2, 1, 3).reshape(SEQS, LEN, HQ)


def reference(queries, attn_keys, attn_values, grad_out, out_weight):
    flat_grad = grad_out.reshape(SEQS * LEN, D)
    dout = jnp.dot(flat_grad, out_weight.T, preferred_element_type=jnp.float32).astype(jnp.bfloat16)
    dout = dout.reshape(SEQS, LEN, HQ)
    attended, grad_q, grad_k, grad_v = lax.map(head_pass, (split_heads(queries), split_heads(attn_keys), split_heads(attn_values), split_heads(dout)))
    attended = join_heads(attended)
    grad_weight = jnp.dot(attended.reshape(SEQS * LEN, HQ).T, flat_grad, preferred_element_type=jnp.float32)
    return join_heads(grad_q), join_heads(grad_k), join_heads(grad_v), grad_weight
```

```python
import math

import jax
import jax.numpy as jnp
from jax import lax
from jax.experimental import pallas as pl
from jax.experimental.pallas import tpu as pltpu
from jax.sharding import PartitionSpec as P

HEAD_DIM = 128
BLOCK = 128
F32 = jnp.float32
BF16 = jnp.bfloat16
NT = (((1,), (1,)), ((), ()))
PARAMS = pltpu.CompilerParams(vmem_limit_bytes=48 * 1024 * 1024)


def dot(a, b):
    return jnp.dot(a, b, preferred_element_type=F32)


def dot_nt(a, b):
    return lax.dot_general(a, b, NT, preferred_element_type=F32)


def pack_qkv_body(q_ref, k_ref, v_ref, out_ref):
    out_ref[0, 0] = q_ref[0]
    out_ref[0, 1] = k_ref[0]
    out_ref[0, 2] = v_ref[0]


def pack_qkv(q, k, v, groups):
    tokens, width = q.shape[1], q.shape[2] // groups
    spec = pl.BlockSpec((1, tokens, width), lambda i: (0, 0, i))
    return pl.pallas_call(
        pack_qkv_body,
        grid=(groups,),
        in_specs=[spec] * 3,
        out_specs=pl.BlockSpec((1, 3, tokens, width), lambda i: (i, 0, 0, 0)),
        out_shape=jax.ShapeDtypeStruct((groups, 3, tokens, width), BF16),
        compiler_params=PARAMS,
    )(q, k, v)


def pack_grad_body(g_ref, a_ref, b_ref):
    for t in range(g_ref.shape[2] // (3 * BLOCK)):
        lo = 3 * BLOCK * t
        a_ref[:, 2 * BLOCK * t : 2 * BLOCK * t + BLOCK] = g_ref[0, :, lo : lo + BLOCK]
        a_ref[:, 2 * BLOCK * t + BLOCK : 2 * BLOCK * (t + 1)] = g_ref[0, :, lo + 2 * BLOCK : lo + 3 * BLOCK]
        b_ref[:, BLOCK * t : BLOCK * (t + 1)] = g_ref[0, :, lo + BLOCK : lo + 2 * BLOCK]


def pack_grad(g):
    tokens, width = g.shape[1:]
    steps = 4
    w = width // steps
    return pl.pallas_call(
        pack_grad_body,
        grid=(steps,),
        in_specs=[pl.BlockSpec((1, tokens, w), lambda i: (0, 0, i))],
        out_specs=[
            pl.BlockSpec((tokens, 2 * w // 3), lambda i: (0, i)),
            pl.BlockSpec((tokens, w // 3), lambda i: (0, i)),
        ],
        out_shape=[
            jax.ShapeDtypeStruct((tokens, 2 * width // 3), BF16),
            jax.ShapeDtypeStruct((tokens, width // 3), BF16),
        ],
        compiler_params=PARAMS,
    )(g)


def unpack_body(x_ref, q_ref, k_ref, v_ref):
    q_ref[0] = x_ref[0, 0]
    k_ref[0] = x_ref[0, 1]
    v_ref[0] = x_ref[0, 2]


def unpack(x):
    groups, _, tokens, width = x.shape
    spec = pl.BlockSpec((1, tokens, width), lambda i: (0, 0, i))
    return pl.pallas_call(
        unpack_body,
        grid=(groups,),
        in_specs=[pl.BlockSpec((1, 3, tokens, width), lambda i: (i, 0, 0, 0))],
        out_specs=[spec] * 3,
        out_shape=[jax.ShapeDtypeStruct((1, tokens, groups * width), BF16)] * 3,
        compiler_params=PARAMS,
    )(x)


def attend_body(x_ref, att_ref, lse_ref, *, step):
    groups, _, tokens, dim = x_ref.shape
    length = groups * tokens
    fold = math.log2(math.e) / dim**0.5
    q = x_ref[:, 0].reshape(length, dim)
    k = x_ref[:, 1].reshape(length, dim)
    vt = x_ref[:, 2].reshape(length, dim).T
    for lo in range(0, length, step):
        s = dot_nt(k, q[lo : lo + step]) * fold
        top = jnp.max(s, axis=0, keepdims=True)
        e = jnp.exp2(s - top)
        total = jnp.sum(e, axis=0, keepdims=True)
        p = (e * (1.0 / total)).astype(BF16)
        att_ref[:, lo : lo + step] = dot(vt, p).astype(BF16)
        lse_ref[0, :, lo : lo + step] = top + jnp.log2(total)


def attend(x):
    groups, _, tokens, width = x.shape
    heads, length = width // HEAD_DIM, groups * tokens
    return pl.pallas_call(
        lambda *r: attend_body(*r, step=256),
        grid=(heads,),
        in_specs=[pl.BlockSpec((groups, 3, tokens, HEAD_DIM), lambda h: (0, 0, 0, h))],
        out_specs=[
            pl.BlockSpec((HEAD_DIM, length), lambda h: (h, 0)),
            pl.BlockSpec((1, 1, length), lambda h: (h, 0, 0)),
        ],
        out_shape=[
            jax.ShapeDtypeStruct((width, length), BF16),
            jax.ShapeDtypeStruct((heads, 1, length), F32),
        ],
        compiler_params=PARAMS,
        cost_estimate=pl.CostEstimate(flops=8 * heads * length * length * HEAD_DIM, transcendentals=heads * length * length, bytes_accessed=4 * 1024 * 1024),
    )(x)


def attend_grad_body(x_ref, do_ref, att_ref, lse_ref, out_ref, dk_ref, dv_ref, *, step):
    groups, _, tokens, dim = x_ref.shape
    length = groups * tokens
    scale = 1.0 / dim**0.5
    fold = math.log2(math.e) * scale
    q = x_ref[:, 0].reshape(length, dim)
    k = x_ref[:, 1].reshape(length, dim)
    v = x_ref[:, 2].reshape(length, dim)
    kt = k.T
    for lo in range(0, length, step):
        qb = q[lo : lo + step]
        do = do_ref[lo : lo + step]
        p = jnp.exp2(dot_nt(k, qb) * fold - lse_ref[0, :, lo : lo + step])
        gp = dot_nt(v, do)
        dot_t = do.astype(F32).T
        delta = jnp.sum(dot_t * att_ref[:, lo : lo + step].astype(F32), axis=0, keepdims=True)
        gs = (p * (gp - delta)).astype(BF16)
        dv = dot(p.astype(BF16), do)
        dk = dot(gs, qb)
        if lo == 0:
            dv_ref[...] = dv
            dk_ref[...] = dk
        else:
            dv_ref[...] += dv
            dk_ref[...] += dk
        dq = (dot(kt, gs) * scale).T.astype(BF16)
        for j in range(step // tokens):
            out_ref[lo // tokens + j, 0] = dq[j * tokens : (j + 1) * tokens]
    out_ref[:, 1] = (dk_ref[...] * scale).astype(BF16).reshape(groups, tokens, dim)
    out_ref[:, 2] = dv_ref[...].astype(BF16).reshape(groups, tokens, dim)


def attend_grad(x, dout, att, lse):
    groups, _, tokens, width = x.shape
    heads, length = width // HEAD_DIM, groups * tokens
    spec = pl.BlockSpec((groups, 3, tokens, HEAD_DIM), lambda h: (0, 0, 0, h))
    return pl.pallas_call(
        lambda *r: attend_grad_body(*r, step=256),
        grid=(heads,),
        in_specs=[
            spec,
            pl.BlockSpec((length, HEAD_DIM), lambda h: (0, h)),
            pl.BlockSpec((HEAD_DIM, length), lambda h: (h, 0)),
            pl.BlockSpec((1, 1, length), lambda h: (h, 0, 0)),
        ],
        out_specs=spec,
        out_shape=jax.ShapeDtypeStruct(x.shape, BF16),
        scratch_shapes=[pltpu.VMEM((length, HEAD_DIM), F32)] * 2,
        compiler_params=PARAMS,
        cost_estimate=pl.CostEstimate(flops=20 * heads * length * length * HEAD_DIM, transcendentals=heads * length * length, bytes_accessed=8 * 1024 * 1024),
    )(x, dout, att, lse)


def chunk_rows(w_ref, first):
    parts = []
    for z in range(0, w_ref.shape[0], 2):
        if first:
            parts += [w_ref[z, 0, :BLOCK], w_ref[z + 1, 0, BLOCK // 2 :]]
        else:
            parts += [w_ref[z, 0, BLOCK:], w_ref[z + 1, 0, : BLOCK // 2]]
    return jnp.concatenate(parts, axis=0)


def dout_body(*refs, first, pieces):
    pos_ref, g_refs, w_ref = refs[0], refs[1 : 1 + pieces], refs[1 + pieces]
    base_ref = None if first else refs[2 + pieces]
    out_ref, acc_ref = refs[-2:]
    y = pl.program_id(0)
    part = dot(jnp.concatenate([g[...] for g in g_refs], axis=0), chunk_rows(w_ref, first))
    tokens = g_refs[0].shape[0]

    @pl.when(y == 0)
    def _():
        acc_ref[...] = part

    @pl.when(y > 0)
    def _():
        acc_ref[...] += part

    @pl.when(y == pl.num_programs(0) - 1)
    def _():
        for p in range(pieces):
            rows = pl.ds(pl.multiple_of(pos_ref[p] * tokens, tokens), tokens)
            value = acc_ref[p * tokens : (p + 1) * tokens]
            if first:
                out_ref[rows] = value
            else:
                out_ref[rows] = (value + base_ref[rows]).astype(BF16)


def dout_chunk(pos, g, w, base):
    first = base is None
    zs, ys, rows, width = w.shape
    tokens, cols = g[0].shape
    length = tokens * len(g)
    whole = pl.BlockSpec((length, width), lambda y: (0, 0))
    return pl.pallas_call(
        lambda *r: dout_body(*r, first=first, pieces=len(g)),
        grid=(ys,),
        in_specs=[pl.BlockSpec(memory_space=pltpu.SMEM)]
        + [pl.BlockSpec((tokens, cols // ys), lambda y: (0, y))] * len(g)
        + [pl.BlockSpec((zs, 1, rows, width), lambda y: (0, y, 0, 0))]
        + ([] if first else [whole]),
        out_specs=whole,
        out_shape=jax.ShapeDtypeStruct((length, width), F32 if first else BF16),
        scratch_shapes=[pltpu.VMEM((length, width), F32)],
        compiler_params=PARAMS,
        cost_estimate=pl.CostEstimate(flops=2 * length * cols * width, transcendentals=0, bytes_accessed=2 * length * cols),
    )(pos, *g, w, *([] if first else [base]))


def term_body(*refs, pieces):
    pos_ref, g_refs, att_ref = refs[0], refs[1 : 1 + pieces], refs[1 + pieces]
    out_ref, own_ref = refs[-2:]
    tokens = g_refs[0].shape[0]

    @pl.when((pl.program_id(0) == 0) & (pl.program_id(1) == 0))
    def _():
        for p in range(pieces):
            cols = pl.ds(pl.multiple_of(pos_ref[p] * tokens, tokens), tokens)
            own_ref[:, p * tokens : (p + 1) * tokens] = att_ref[:, cols]

    out_ref[0] = dot(own_ref[...], jnp.concatenate([g[...] for g in g_refs], axis=0)).astype(BF16)


def term_chunk(pos, g, att, ys):
    tokens, cols = g[0].shape
    width, length = att.shape
    step = 512
    per = cols // ys // step
    return pl.pallas_call(
        lambda *r: term_body(*r, pieces=len(g)),
        grid=(ys, per),
        in_specs=[pl.BlockSpec(memory_space=pltpu.SMEM)]
        + [pl.BlockSpec((tokens, step), lambda y, j: (0, y * per + j))] * len(g)
        + [pl.BlockSpec((width, length), lambda y, j: (0, 0))],
        out_specs=pl.BlockSpec((1, width, step), lambda y, j: (y, 0, j)),
        out_shape=jax.ShapeDtypeStruct((ys, width, cols // ys), BF16),
        scratch_shapes=[pltpu.VMEM((width, length), BF16)],
        compiler_params=PARAMS,
        cost_estimate=pl.CostEstimate(flops=2 * length * cols * width, transcendentals=0, bytes_accessed=2 * (length + width) * cols),
    )(pos, *g, att)


def fold_body(z_ref, x_ref, *out_refs):
    ways = len(out_refs)
    cols = x_ref.shape[2]
    total = x_ref[0].astype(F32)
    for i in range(1, x_ref.shape[0]):
        total = total + x_ref[i].astype(F32)
    flat = total.T
    step = cols // ways
    for z in range(ways):
        value = flat[z * step : (z + 1) * step].astype(BF16)
        away = lax.rem(z - z_ref[0] + ways, ways)
        for d in range(ways):

            @pl.when(away == d)
            def _(d=d, value=value):
                out_refs[d][...] = value


def fold(zi, x, ways):
    ys, width, cols = x.shape
    piece = jax.ShapeDtypeStruct((cols // ways, width), BF16)
    vmem = pl.BlockSpec(memory_space=pltpu.VMEM)
    return pl.pallas_call(
        fold_body,
        in_specs=[pl.BlockSpec(memory_space=pltpu.SMEM), vmem],
        out_specs=[vmem] * ways,
        out_shape=[piece] * ways,
        compiler_params=PARAMS,
    )(zi, x)


def finish_body(odd_ref, *refs):
    out_ref = refs[-1]
    ways = (len(refs) - 1) // 2
    odd = odd_ref[0]
    for refs_here, even_at, odd_at in ((refs[:ways], 0, BLOCK // 2), (refs[ways : 2 * ways], BLOCK, 0)):
        total = refs_here[0][...].astype(F32)
        for r in refs_here[1:]:
            total = total + r[...].astype(F32)
        at = pl.multiple_of(jnp.where(odd == 1, odd_at, even_at), BLOCK // 2)
        out_ref[pl.ds(at, total.shape[0])] = total


def finish(odd, first, second):
    width = first[0].shape[1]
    rows = first[0].shape[0] + second[0].shape[0]
    vmem = pl.BlockSpec(memory_space=pltpu.VMEM)
    return pl.pallas_call(
        finish_body,
        in_specs=[pl.BlockSpec(memory_space=pltpu.SMEM)] + [vmem] * (len(first) + len(second)),
        out_specs=vmem,
        out_shape=jax.ShapeDtypeStruct((rows, width), F32),
        compiler_params=PARAMS,
    )(odd, *first, *second)


def solution(mesh):
    groups, spread = mesh.shape["seq"], mesh.shape["fsdp"]
    ys, zs = 4, spread // 4
    chips = groups // 2
    y_groups = [[y * zs + z for y in range(ys)] for z in range(zs)]
    z_groups = [[y * zs + z for z in range(zs)] for y in range(ys)]

    def along_x(a, d):
        return lax.ppermute(a, "seq", [(i, (i + 2 * d) % groups) for i in range(groups)])

    def swap(a):
        return lax.ppermute(a, "seq", [(i, i ^ 1) for i in range(groups)])

    def along_z(a, d):
        return lax.ppermute(a, "fsdp", [(y * zs + z, y * zs + (z + d) % zs) for y in range(ys) for z in range(zs)])

    def gather_chunk(a):
        same = [a] + [along_x(a, d) for d in (1, -1, 2)]
        return same + [swap(x) for x in same]

    def exchange(term, zi):
        got = lax.all_to_all(term, "fsdp", 0, 0, tiled=True, axis_index_groups=y_groups)
        parts = fold(zi, got, zs)
        return [parts[0]] + [along_z(parts[d], d) for d in range(1, zs)]

    def shards(queries, attn_keys, attn_values, grad_out, out_weight):
        me = lax.axis_index("seq")
        zi = lax.rem(lax.axis_index("fsdp"), zs)
        x, core = me // 2, lax.rem(me, 2)
        near = [lax.rem(x + chips - d, chips) * 2 for d in (0, 1, -1, 2)]
        pos = jnp.stack([n + core for n in near] + [n + 1 - core for n in near]).astype(jnp.int32)
        zi = zi.astype(jnp.int32).reshape(1)

        chunk_a, chunk_b = pack_grad(grad_out)
        packed = pack_qkv(queries, attn_keys, attn_values, groups)
        heads = lax.all_to_all(packed, "seq", 0, 0, tiled=True)
        rows = lax.all_gather(out_weight.T, "fsdp", axis=0, axis_index_groups=y_groups)
        weight = lax.all_gather(rows, "fsdp", axis=0, axis_index_groups=z_groups)
        got_a = gather_chunk(chunk_a)
        got_b = gather_chunk(chunk_b)

        att, lse = attend(heads)
        term_a = term_chunk(pos, got_a, att, ys)
        sums_a = exchange(term_a, zi)
        part = dout_chunk(pos, got_a, weight, None)
        dout = dout_chunk(pos, got_b, weight, part)
        term_b = term_chunk(pos, got_b, att, ys)
        grads = attend_grad(heads, dout, att, lse)
        sums_b = exchange(term_b, zi)
        back = lax.all_to_all(grads, "seq", 0, 0, tiled=True)
        grad_q, grad_k, grad_v = unpack(back)
        grad_weight = finish(lax.rem(zi, 2), sums_a, sums_b).T
        return grad_q, grad_k, grad_v, grad_weight

    tokens, weights = P("fsdp", "seq", None), P("seq", "fsdp")
    return jax.shard_map(
        shards,
        mesh=mesh,
        in_specs=(tokens, tokens, tokens, tokens, weights),
        out_specs=(tokens, tokens, tokens, weights),
        check_vma=False,
    )
```

```python
import math

import jax
import jax.numpy as jnp
from jax import lax
from jax.experimental import pallas as pl
from jax.experimental.pallas import tpu as pltpu
from jax.sharding import PartitionSpec as P

HEAD_DIM = 128
BLOCK = 128
F32 = jnp.float32
BF16 = jnp.bfloat16
NT = (((1,), (1,)), ((), ()))
PARAMS = pltpu.CompilerParams(vmem_limit_bytes=24 * 1024 * 1024)
FREE = pl.CostEstimate(flops=0, transcendentals=0, bytes_accessed=0)
LONG = pl.CostEstimate(flops=10**11, transcendentals=0, bytes_accessed=10**8)
ANY = pl.BlockSpec(memory_space=pl.ANY)
VMEM = pl.BlockSpec(memory_space=pltpu.VMEM)
SMEM = pl.BlockSpec(memory_space=pltpu.SMEM)


def dot(a, b):
    return jnp.dot(a, b, preferred_element_type=F32)


def dot_nt(a, b):
    return lax.dot_general(a, b, NT, preferred_element_type=F32)


def run_copies(pairs, sems):
    copies = [pltpu.make_async_copy(src, dst, sems.at[i]) for i, (src, dst) in enumerate(pairs)]
    for c in copies:
        c.start()
    for c in copies:
        c.wait()


def pack_heads_body(q_ref, k_ref, v_ref, out_ref, sems):
    groups, _, _, width = out_ref.shape
    run_copies(
        [
            (ref.at[0, :, i * width : (i + 1) * width], out_ref.at[i, j])
            for i in range(groups)
            for j, ref in enumerate((q_ref, k_ref, v_ref))
        ],
        sems,
    )


def pack_heads(q, k, v, groups):
    tokens, width = q.shape[1], q.shape[2] // groups
    return pl.pallas_call(
        pack_heads_body,
        in_specs=[ANY] * 3,
        out_specs=ANY,
        out_shape=jax.ShapeDtypeStruct((groups, 3, tokens, width), BF16),
        scratch_shapes=[pltpu.SemaphoreType.DMA((3 * groups,))],
        compiler_params=PARAMS,
        cost_estimate=FREE,
    )(q, k, v)


def unpack_heads_body(x_ref, q_ref, k_ref, v_ref, sems):
    groups, _, _, width = x_ref.shape
    run_copies(
        [
            (x_ref.at[i, j], ref.at[0, :, i * width : (i + 1) * width])
            for i in range(groups)
            for j, ref in enumerate((q_ref, k_ref, v_ref))
        ],
        sems,
    )


def unpack_heads(x):
    groups, _, tokens, width = x.shape
    return pl.pallas_call(
        unpack_heads_body,
        in_specs=[ANY],
        out_specs=[ANY] * 3,
        out_shape=[jax.ShapeDtypeStruct((1, tokens, groups * width), BF16)] * 3,
        scratch_shapes=[pltpu.SemaphoreType.DMA((3 * groups,))],
        compiler_params=PARAMS,
        cost_estimate=FREE,
    )(x)


def pack_grad_body(g_ref, a_ref, b_ref, sems):
    def cols(ref, at):
        return ref.at[:, at * BLOCK : (at + 1) * BLOCK]

    pairs = []
    for t in range(g_ref.shape[2] // (3 * BLOCK)):
        pairs += [
            (cols(g_ref.at[0], 3 * t), cols(a_ref, 2 * t)),
            (cols(g_ref.at[0], 3 * t + 2), cols(a_ref, 2 * t + 1)),
            (cols(g_ref.at[0], 3 * t + 1), cols(b_ref, t)),
        ]
    run_copies(pairs, sems)


def pack_grad(g):
    tokens, width = g.shape[1:]
    return pl.pallas_call(
        pack_grad_body,
        in_specs=[ANY],
        out_specs=[ANY] * 2,
        out_shape=[
            jax.ShapeDtypeStruct((tokens, 2 * width // 3), BF16),
            jax.ShapeDtypeStruct((tokens, width // 3), BF16),
        ],
        scratch_shapes=[pltpu.SemaphoreType.DMA((width // BLOCK,))],
        compiler_params=PARAMS,
        cost_estimate=FREE,
    )(g)


def attend_body(x_ref, att_ref, lse_ref, *, step):
    groups, _, tokens, width = x_ref.shape
    length, dim = groups * tokens, HEAD_DIM
    fold = math.log2(math.e) / dim**0.5
    for h in range(width // dim):
        own = slice(h * dim, (h + 1) * dim)
        q = x_ref[:, 0, :, own].reshape(length, dim)
        k = x_ref[:, 1, :, own].reshape(length, dim)
        vt = x_ref[:, 2, :, own].reshape(length, dim).T
        for lo in range(0, length, step):
            s = dot_nt(k, q[lo : lo + step])
            top = jnp.max(s, axis=0, keepdims=True) * fold
            e = jnp.exp2(s * fold - top)
            total = jnp.sum(e, axis=0, keepdims=True)
            att_ref[own, lo : lo + step] = (dot(vt, e.astype(BF16)) * (1.0 / total)).astype(BF16)
            lse_ref[h, :, lo : lo + step] = top + jnp.log2(total)


def attend(x):
    groups, _, tokens, width = x.shape
    heads, length = width // HEAD_DIM, groups * tokens
    return pl.pallas_call(
        lambda *r: attend_body(*r, step=256),
        in_specs=[VMEM],
        out_specs=[VMEM] * 2,
        out_shape=[
            jax.ShapeDtypeStruct((width, length), BF16),
            jax.ShapeDtypeStruct((heads, 1, length), F32),
        ],
        compiler_params=PARAMS,
        cost_estimate=FREE,
    )(x)


def attend_grad_body(x_ref, do_ref, att_ref, lse_ref, out_ref, dk_ref, dv_ref, *, step):
    groups, _, tokens, width = x_ref.shape
    length, dim = groups * tokens, HEAD_DIM
    scale = 1.0 / dim**0.5
    fold = math.log2(math.e) * scale
    for h in range(width // dim):
        own = slice(h * dim, (h + 1) * dim)
        q = x_ref[:, 0, :, own].reshape(length, dim)
        k = x_ref[:, 1, :, own].reshape(length, dim)
        v = x_ref[:, 2, :, own].reshape(length, dim)
        kt = k.T
        for lo in range(0, length, step):
            qb = q[lo : lo + step]
            do = do_ref[lo : lo + step, own]
            p = jnp.exp2(dot_nt(k, qb) * fold - lse_ref[h, :, lo : lo + step])
            gp = dot_nt(v, do)
            do_t = do.astype(F32).T
            delta = jnp.sum(do_t * att_ref[own, lo : lo + step].astype(F32), axis=0, keepdims=True)
            gs = (p * (gp - delta)).astype(BF16)
            dv = dot(p.astype(BF16), do)
            dk = dot(gs, qb)
            if lo == 0:
                dv_ref[...] = dv
                dk_ref[...] = dk
            else:
                dv_ref[...] += dv
                dk_ref[...] += dk
            dq = (dot(kt, gs) * scale).T.astype(BF16)
            for j in range(step // tokens):
                out_ref[lo // tokens + j, 0, :, own] = dq[j * tokens : (j + 1) * tokens]
        out_ref[:, 1, :, own] = (dk_ref[...] * scale).astype(BF16).reshape(groups, tokens, dim)
        out_ref[:, 2, :, own] = dv_ref[...].astype(BF16).reshape(groups, tokens, dim)


def attend_grad(x, dout, att, lse):
    groups, _, tokens, _ = x.shape
    return pl.pallas_call(
        lambda *r: attend_grad_body(*r, step=256),
        in_specs=[VMEM] * 4,
        out_specs=VMEM,
        out_shape=jax.ShapeDtypeStruct(x.shape, BF16),
        scratch_shapes=[pltpu.VMEM((groups * tokens, HEAD_DIM), F32)] * 2,
        compiler_params=PARAMS,
        cost_estimate=FREE,
    )(x, dout, att, lse)


def chunk_rows(w_ref, y, first):
    parts = []
    for z in range(0, w_ref.shape[1], 2):
        if first:
            parts += [w_ref[y, z, :BLOCK], w_ref[y, z + 1, BLOCK // 2 :]]
        else:
            parts += [w_ref[y, z, BLOCK:], w_ref[y, z + 1, : BLOCK // 2]]
    return jnp.concatenate(parts, axis=0)


def dout_body(*refs, pieces):
    pos_ref, w_ref, out_ref, acc_ref = refs[0], refs[-3], refs[-2], refs[-1]
    a_refs, b_refs = refs[1 : 1 + pieces], refs[1 + pieces : 1 + 2 * pieces]
    tokens = a_refs[0].shape[0]
    ys = w_ref.shape[0]
    for y in range(ys):
        part = None
        for g_refs, first in ((a_refs, True), (b_refs, False)):
            step = g_refs[0].shape[1] // ys
            rows = jnp.concatenate([g[:, y * step : (y + 1) * step] for g in g_refs], axis=0)
            more = dot(rows, chunk_rows(w_ref, y, first))
            part = more if part is None else part + more
        if y == 0:
            acc_ref[...] = part
        elif y < ys - 1:
            acc_ref[...] += part
        else:
            for p in range(pieces):
                own = slice(p * tokens, (p + 1) * tokens)
                at = pl.ds(pl.multiple_of(pos_ref[p] * tokens, tokens), tokens)
                out_ref[at] = (acc_ref[own] + part[own]).astype(BF16)


def find_dout(pos, got_a, got_b, w):
    shape = (got_a[0].shape[0] * len(got_a), w.shape[3])
    return pl.pallas_call(
        lambda *r: dout_body(*r, pieces=len(got_a)),
        in_specs=[SMEM] + [VMEM] * (2 * len(got_a) + 1),
        out_specs=VMEM,
        out_shape=jax.ShapeDtypeStruct(shape, BF16),
        scratch_shapes=[pltpu.VMEM(shape, F32)],
        compiler_params=PARAMS,
        cost_estimate=LONG,
    )(pos, *got_a, *got_b, w)


def term_body(*refs, pieces, step):
    pos_ref, g_refs, att_ref = refs[0], refs[1 : 1 + pieces], refs[1 + pieces]
    out_ref, own_ref = refs[-2:]
    tokens = g_refs[0].shape[0]
    ys, _, cols = out_ref.shape
    for p in range(pieces):
        at = pl.ds(pl.multiple_of(pos_ref[p] * tokens, tokens), tokens)
        own_ref[:, p * tokens : (p + 1) * tokens] = att_ref[:, at]
    for y in range(ys):
        for lo in range(0, cols, step):
            at = y * cols + lo
            rows = jnp.concatenate([g[:, at : at + step] for g in g_refs], axis=0)
            out_ref[y, :, lo : lo + step] = dot(own_ref[...], rows).astype(BF16)


def term_chunk(pos, g, att, ys):
    cols = g[0].shape[1]
    width = att.shape[0]
    return pl.pallas_call(
        lambda *r: term_body(*r, pieces=len(g), step=512),
        in_specs=[SMEM] + [VMEM] * (len(g) + 1),
        out_specs=VMEM,
        out_shape=jax.ShapeDtypeStruct((ys, width, cols // ys), BF16),
        scratch_shapes=[pltpu.VMEM(att.shape, BF16)],
        compiler_params=PARAMS,
        cost_estimate=FREE,
    )(pos, *g, att)


def fold_body(z_ref, x_ref, *out_refs):
    ways = len(out_refs)
    cols = x_ref.shape[2]
    total = x_ref[0].astype(F32)
    for i in range(1, x_ref.shape[0]):
        total = total + x_ref[i].astype(F32)
    flat = total.T
    step = cols // ways
    for z in range(ways):
        value = flat[z * step : (z + 1) * step].astype(BF16)
        away = lax.rem(z - z_ref[0] + ways, ways)
        for d in range(ways):

            @pl.when(away == d)
            def _(d=d, value=value):
                out_refs[d][...] = value


def fold(zi, x, ways):
    ys, width, cols = x.shape
    piece = jax.ShapeDtypeStruct((cols // ways, width), BF16)
    return pl.pallas_call(
        fold_body,
        in_specs=[pl.BlockSpec(memory_space=pltpu.SMEM), VMEM],
        out_specs=[VMEM] * ways,
        out_shape=[piece] * ways,
        compiler_params=PARAMS,
        cost_estimate=FREE,
    )(zi, x)


def finish_body(odd_ref, *refs):
    out_ref = refs[-1]
    ways = (len(refs) - 1) // 2
    odd = odd_ref[0]
    for refs_here, even_at, odd_at in ((refs[:ways], 0, BLOCK // 2), (refs[ways : 2 * ways], BLOCK, 0)):
        total = refs_here[0][...].astype(F32)
        for r in refs_here[1:]:
            total = total + r[...].astype(F32)
        at = pl.multiple_of(jnp.where(odd == 1, odd_at, even_at), BLOCK // 2)
        out_ref[pl.ds(at, total.shape[0])] = total


def finish(odd, first, second):
    width = first[0].shape[1]
    rows = first[0].shape[0] + second[0].shape[0]
    return pl.pallas_call(
        finish_body,
        in_specs=[SMEM] + [VMEM] * (len(first) + len(second)),
        out_specs=VMEM,
        out_shape=jax.ShapeDtypeStruct((rows, width), F32),
        compiler_params=PARAMS,
        cost_estimate=FREE,
    )(odd, *first, *second)


def solution(mesh):
    groups, spread = mesh.shape["seq"], mesh.shape["fsdp"]
    ys, zs = 4, spread // 4
    chips = groups // 2
    y_groups = [[y * zs + z for y in range(ys)] for z in range(zs)]
    z_groups = [[y * zs + z for z in range(zs)] for y in range(ys)]

    def along_x(a, d):
        return lax.ppermute(a, "seq", [(i, (i + 2 * d) % groups) for i in range(groups)])

    def swap(a):
        return lax.ppermute(a, "seq", [(i, i ^ 1) for i in range(groups)])

    def along_z(a, d):
        return lax.ppermute(a, "fsdp", [(y * zs + z, y * zs + (z + d) % zs) for y in range(ys) for z in range(zs)])

    def along_y(a, d):
        return lax.ppermute(a, "fsdp", [(y * zs + z, (y + d) % ys * zs + z) for y in range(ys) for z in range(zs)])

    def after(a, *others):
        return lax.optimization_barrier((a, *others))[0]

    def scatter_z(got, zi):
        parts = fold(zi, got, zs)
        return [parts[0]] + [along_z(parts[d], d) for d in range(1, zs)]

    def shards(queries, attn_keys, attn_values, grad_out, out_weight):
        me = lax.axis_index("seq")
        f = lax.axis_index("fsdp")
        x, core, yi, zi = me // 2, me % 2, f // zs, f % zs
        near = [(x - d) % chips * 2 for d in (0, 1, -1, 2)]
        pos = jnp.stack([n + core for n in near] + [n + 1 - core for n in near]).astype(jnp.int32)
        z_index = zi.astype(jnp.int32).reshape(1)

        column = lax.all_gather(out_weight.T, "fsdp", axis=0, axis_index_groups=z_groups)
        weight = lax.all_gather(column, "fsdp", axis=0, axis_index_groups=y_groups)

        chunk_a, chunk_b = pack_grad(grad_out)
        packed = pack_heads(after(queries, chunk_a), attn_keys, attn_values, groups)
        same_a = [chunk_a] + [along_x(chunk_a, d) for d in (1, -1, 2)]
        heads = lax.all_to_all(packed, "seq", 0, 0, tiled=True)
        got_a = same_a + [swap(a) for a in same_a]
        same_b = [chunk_b] + [along_x(after(chunk_b, same_a[i]), d) for i, d in ((1, 1), (2, -1), (3, 2))]

        att, lse = attend(after(heads, *got_a))
        term_a = term_chunk(pos, got_a, att, ys)
        got_b = same_b + [swap(after(b, term_a)) for b in same_b]
        fold_a = lax.all_to_all(term_a, "fsdp", 0, 0, tiled=True, axis_index_groups=y_groups)
        term_b = term_chunk(after(pos, term_a), got_b, att, ys)
        dout = find_dout(after(pos, term_b), got_a, got_b, weight)
        grads = attend_grad(heads, dout, att, lse)
        back = lax.all_to_all(grads, "seq", 0, 0, tiled=True)

        def own(d):
            return lax.dynamic_index_in_dim(term_b, (yi + d) % ys, 0, keepdims=False)

        fold_b = jnp.stack([own(0)] + [along_y(own(d), d) for d in (1, -1, 2)])
        sums_a = scatter_z(fold_a, z_index)
        sums_b = scatter_z(fold_b, z_index)
        grad_q, grad_k, grad_v = unpack_heads(back)
        grad_weight = finish(z_index % 2, sums_a, sums_b).T
        return grad_q, grad_k, grad_v, grad_weight

    tokens, weights = P("fsdp", "seq", None), P("seq", "fsdp")
    return jax.shard_map(
        shards,
        mesh=mesh,
        in_specs=(tokens, tokens, tokens, tokens, weights),
        out_specs=(tokens, tokens, tokens, weights),
        check_vma=False,
    )
```

```python
import math

import jax
import jax.numpy as jnp
from jax import lax
from jax.experimental import pallas as pl
from jax.experimental.pallas import tpu as pltpu
from jax.sharding import PartitionSpec as P

HEAD_DIM = 128
BLOCK = 128
F32 = jnp.float32
BF16 = jnp.bfloat16
NT = (((1,), (1,)), ((), ()))
PARAMS = pltpu.CompilerParams(vmem_limit_bytes=24 * 1024 * 1024)
FREE = pl.CostEstimate(flops=0, transcendentals=0, bytes_accessed=0)
LONG = pl.CostEstimate(flops=10**11, transcendentals=0, bytes_accessed=10**8)
ANY = pl.BlockSpec(memory_space=pl.ANY)
VMEM = pl.BlockSpec(memory_space=pltpu.VMEM)
SMEM = pl.BlockSpec(memory_space=pltpu.SMEM)


def dot(a, b):
    return jnp.dot(a, b, preferred_element_type=F32)


def dot_nt(a, b):
    return lax.dot_general(a, b, NT, preferred_element_type=F32)


def run_copies(pairs, sems):
    copies = [pltpu.make_async_copy(src, dst, sems.at[i]) for i, (src, dst) in enumerate(pairs)]
    for c in copies:
        c.start()
    for c in copies:
        c.wait()


def pack_heads_body(q_ref, k_ref, v_ref, out_ref, sems):
    groups, _, _, width = out_ref.shape
    run_copies(
        [
            (ref.at[0, :, i * width : (i + 1) * width], out_ref.at[i, j])
            for i in range(groups)
            for j, ref in enumerate((q_ref, k_ref, v_ref))
        ],
        sems,
    )


def pack_heads(q, k, v, groups):
    tokens, width = q.shape[1], q.shape[2] // groups
    return pl.pallas_call(
        pack_heads_body,
        in_specs=[ANY] * 3,
        out_specs=ANY,
        out_shape=jax.ShapeDtypeStruct((groups, 3, tokens, width), BF16),
        scratch_shapes=[pltpu.SemaphoreType.DMA((3 * groups,))],
        compiler_params=PARAMS,
        cost_estimate=FREE,
    )(q, k, v)


def unpack_heads_body(x_ref, q_ref, k_ref, v_ref, sems):
    groups, _, _, width = x_ref.shape
    run_copies(
        [
            (x_ref.at[i, j], ref.at[0, :, i * width : (i + 1) * width])
            for i in range(groups)
            for j, ref in enumerate((q_ref, k_ref, v_ref))
        ],
        sems,
    )


def unpack_heads(x):
    groups, _, tokens, width = x.shape
    return pl.pallas_call(
        unpack_heads_body,
        in_specs=[ANY],
        out_specs=[ANY] * 3,
        out_shape=[jax.ShapeDtypeStruct((1, tokens, groups * width), BF16)] * 3,
        scratch_shapes=[pltpu.SemaphoreType.DMA((3 * groups,))],
        compiler_params=PARAMS,
        cost_estimate=FREE,
    )(x)


def pack_grad_body(g_ref, a_ref, b_ref, sems):
    def cols(ref, at):
        return ref.at[:, at * BLOCK : (at + 1) * BLOCK]

    pairs = []
    for t in range(g_ref.shape[2] // (3 * BLOCK)):
        pairs += [
            (cols(g_ref.at[0], 3 * t), cols(a_ref, 2 * t)),
            (cols(g_ref.at[0], 3 * t + 2), cols(a_ref, 2 * t + 1)),
            (cols(g_ref.at[0], 3 * t + 1), cols(b_ref, t)),
        ]
    run_copies(pairs, sems)


def pack_grad(g):
    tokens, width = g.shape[1:]
    return pl.pallas_call(
        pack_grad_body,
        in_specs=[ANY],
        out_specs=[ANY] * 2,
        out_shape=[
            jax.ShapeDtypeStruct((tokens, 2 * width // 3), BF16),
            jax.ShapeDtypeStruct((tokens, width // 3), BF16),
        ],
        scratch_shapes=[pltpu.SemaphoreType.DMA((width // BLOCK,))],
        compiler_params=PARAMS,
        cost_estimate=FREE,
    )(g)


def attend_body(x_ref, att_ref, lse_ref, *, step):
    groups, _, tokens, width = x_ref.shape
    length, dim = groups * tokens, HEAD_DIM
    fold = math.log2(math.e) / dim**0.5
    for h in range(width // dim):
        own = slice(h * dim, (h + 1) * dim)
        q = x_ref[:, 0, :, own].reshape(length, dim)
        k = x_ref[:, 1, :, own].reshape(length, dim)
        vt = x_ref[:, 2, :, own].reshape(length, dim).T
        for lo in range(0, length, step):
            s = dot_nt(k, q[lo : lo + step])
            top = jnp.max(s, axis=0, keepdims=True) * fold
            e = jnp.exp2(s * fold - top)
            total = jnp.sum(e, axis=0, keepdims=True)
            att_ref[own, lo : lo + step] = (dot(vt, e.astype(BF16)) * (1.0 / total)).astype(BF16)
            lse_ref[h, :, lo : lo + step] = top + jnp.log2(total)


def attend(x):
    groups, _, tokens, width = x.shape
    heads, length = width // HEAD_DIM, groups * tokens
    return pl.pallas_call(
        lambda *r: attend_body(*r, step=256),
        in_specs=[VMEM],
        out_specs=[VMEM] * 2,
        out_shape=[
            jax.ShapeDtypeStruct((width, length), BF16),
            jax.ShapeDtypeStruct((heads, 1, length), F32),
        ],
        compiler_params=PARAMS,
        cost_estimate=FREE,
    )(x)


def attend_grad_body(x_ref, do_ref, att_ref, lse_ref, out_ref, dk_ref, dv_ref, *, step):
    groups, _, tokens, width = x_ref.shape
    length, dim = groups * tokens, HEAD_DIM
    scale = 1.0 / dim**0.5
    fold = math.log2(math.e) * scale
    for h in range(width // dim):
        own = slice(h * dim, (h + 1) * dim)
        q = x_ref[:, 0, :, own].reshape(length, dim)
        k = x_ref[:, 1, :, own].reshape(length, dim)
        v = x_ref[:, 2, :, own].reshape(length, dim)
        kt = k.T
        for lo in range(0, length, step):
            qb = q[lo : lo + step]
            do = do_ref[lo : lo + step, own]
            p = jnp.exp2(dot_nt(k, qb) * fold - lse_ref[h, :, lo : lo + step])
            gp = dot_nt(v, do)
            do_t = do.astype(F32).T
            delta = jnp.sum(do_t * att_ref[own, lo : lo + step].astype(F32), axis=0, keepdims=True)
            gs = (p * (gp - delta)).astype(BF16)
            dv = dot(p.astype(BF16), do)
            dk = dot(gs, qb)
            if lo == 0:
                dv_ref[...] = dv
                dk_ref[...] = dk
            else:
                dv_ref[...] += dv
                dk_ref[...] += dk
            dq = (dot(kt, gs) * scale).T.astype(BF16)
            for j in range(step // tokens):
                out_ref[lo // tokens + j, 0, :, own] = dq[j * tokens : (j + 1) * tokens]
        out_ref[:, 1, :, own] = (dk_ref[...] * scale).astype(BF16).reshape(groups, tokens, dim)
        out_ref[:, 2, :, own] = dv_ref[...].astype(BF16).reshape(groups, tokens, dim)


def attend_grad(x, dout, att, lse):
    groups, _, tokens, _ = x.shape
    return pl.pallas_call(
        lambda *r: attend_grad_body(*r, step=256),
        in_specs=[VMEM] * 4,
        out_specs=VMEM,
        out_shape=jax.ShapeDtypeStruct(x.shape, BF16),
        scratch_shapes=[pltpu.VMEM((groups * tokens, HEAD_DIM), F32)] * 2,
        compiler_params=PARAMS,
        cost_estimate=FREE,
    )(x, dout, att, lse)


def chunk_rows(w_ref, y, first):
    parts = []
    for z in range(0, w_ref.shape[1], 2):
        if first:
            parts += [w_ref[y, z, :BLOCK], w_ref[y, z + 1, BLOCK // 2 :]]
        else:
            parts += [w_ref[y, z, BLOCK:], w_ref[y, z + 1, : BLOCK // 2]]
    return jnp.concatenate(parts, axis=0)


def dout_body(*refs, pieces):
    pos_ref, w_ref, out_ref, acc_ref = refs[0], refs[-3], refs[-2], refs[-1]
    a_refs, b_refs = refs[1 : 1 + pieces], refs[1 + pieces : 1 + 2 * pieces]
    tokens = a_refs[0].shape[0]
    ys = w_ref.shape[0]
    for y in range(ys):
        part = None
        for g_refs, first in ((a_refs, True), (b_refs, False)):
            step = g_refs[0].shape[1] // ys
            rows = jnp.concatenate([g[:, y * step : (y + 1) * step] for g in g_refs], axis=0)
            more = dot(rows, chunk_rows(w_ref, y, first))
            part = more if part is None else part + more
        if y == 0:
            acc_ref[...] = part
        elif y < ys - 1:
            acc_ref[...] += part
        else:
            for p in range(pieces):
                own = slice(p * tokens, (p + 1) * tokens)
                at = pl.ds(pl.multiple_of(pos_ref[p] * tokens, tokens), tokens)
                out_ref[at] = (acc_ref[own] + part[own]).astype(BF16)


def find_dout(pos, got_a, got_b, w):
    shape = (got_a[0].shape[0] * len(got_a), w.shape[3])
    return pl.pallas_call(
        lambda *r: dout_body(*r, pieces=len(got_a)),
        in_specs=[SMEM] + [VMEM] * (2 * len(got_a) + 1),
        out_specs=VMEM,
        out_shape=jax.ShapeDtypeStruct(shape, BF16),
        scratch_shapes=[pltpu.VMEM(shape, F32)],
        compiler_params=PARAMS,
        cost_estimate=LONG,
    )(pos, *got_a, *got_b, w)


def own_order(pos_ref, att_ref, own_ref, pieces):
    tokens = att_ref.shape[1] // pieces
    for p in range(pieces):
        at = pl.ds(pl.multiple_of(pos_ref[p] * tokens, tokens), tokens)
        own_ref[:, p * tokens : (p + 1) * tokens] = att_ref[:, at]


def term_a_body(*refs, pieces, step):
    pos_ref, g_refs, att_ref = refs[0], refs[1 : 1 + pieces], refs[1 + pieces]
    out_ref, own_ref = refs[-2:]
    ys, _, cols = out_ref.shape
    own_order(pos_ref, att_ref, own_ref, pieces)
    for y in range(ys):
        for lo in range(0, cols, step):
            at = y * cols + lo
            rows = jnp.concatenate([g[:, at : at + step] for g in g_refs], axis=0)
            out_ref[y, :, lo : lo + step] = dot(own_ref[...], rows).astype(BF16)


def find_term_a(pos, g, att, ys):
    cols = g[0].shape[1]
    width = att.shape[0]
    return pl.pallas_call(
        lambda *r: term_a_body(*r, pieces=len(g), step=512),
        in_specs=[SMEM] + [VMEM] * (len(g) + 1),
        out_specs=VMEM,
        out_shape=jax.ShapeDtypeStruct((ys, width, cols // ys), BF16),
        scratch_shapes=[pltpu.VMEM(att.shape, BF16)],
        compiler_params=PARAMS,
        cost_estimate=FREE,
    )(pos, *g, att)


def term_b_body(*refs, pieces, ways):
    pos_ref, z_ref, g_refs, att_ref = refs[0], refs[1], refs[2 : 2 + pieces], refs[2 + pieces]
    out_refs, own_ref, all_ref = refs[-2 - ways : -2], refs[-2], refs[-1]
    _, ys, rows_each, _ = all_ref.shape
    step = ways * rows_each
    own_order(pos_ref, att_ref, own_ref, pieces)
    for y in range(ys):
        rows = jnp.concatenate([g[:, y * step : (y + 1) * step] for g in g_refs], axis=0)
        flat = dot(own_ref[...], rows).T.astype(BF16)
        for z in range(ways):
            all_ref[z, y] = flat[z * rows_each : (z + 1) * rows_each]
    for d in range(ways):
        out_refs[d][...] = all_ref[lax.rem(z_ref[0] + d, ways)]


def find_term_b(pos, z_index, g, att, ys, zs):
    cols = g[0].shape[1]
    width = att.shape[0]
    piece = (ys, cols // ys // zs, width)
    return pl.pallas_call(
        lambda *r: term_b_body(*r, pieces=len(g), ways=zs),
        in_specs=[SMEM] * 2 + [VMEM] * (len(g) + 1),
        out_specs=[VMEM] * zs,
        out_shape=[jax.ShapeDtypeStruct(piece, BF16)] * zs,
        scratch_shapes=[pltpu.VMEM(att.shape, BF16), pltpu.VMEM((zs, *piece), BF16)],
        compiler_params=PARAMS,
        cost_estimate=FREE,
    )(pos, z_index, *g, att)


def total_of(values):
    total = values[0].astype(F32)
    for v in values[1:]:
        total = total + v.astype(F32)
    return total


def fold_a_body(z_ref, x_ref, *refs):
    out_refs, all_ref = refs[:-1], refs[-1]
    ways = len(out_refs)
    step = x_ref.shape[2] // ways
    for z in range(ways):
        own = slice(z * step, (z + 1) * step)
        all_ref[z] = total_of([x_ref[i, :, own] for i in range(x_ref.shape[0])]).T.astype(BF16)
    for d in range(ways):
        out_refs[d][...] = all_ref[lax.rem(z_ref[0] + d, ways)]


def fold_a(z_index, x, ways):
    _, width, cols = x.shape
    piece = (cols // ways, width)
    return pl.pallas_call(
        fold_a_body,
        in_specs=[SMEM, VMEM],
        out_specs=[VMEM] * ways,
        out_shape=[jax.ShapeDtypeStruct(piece, BF16)] * ways,
        scratch_shapes=[pltpu.VMEM((ways, *piece), BF16)],
        compiler_params=PARAMS,
        cost_estimate=LONG,
    )(z_index, x)


def fold_b_body(y_ref, *refs, count, moves):
    in_refs, out_refs, all_ref = refs[:count], refs[count:-1], refs[-1]
    ways = all_ref.shape[0]
    for y in range(ways):
        all_ref[y] = total_of([r[y] for r in in_refs])
    for ref, d in zip(out_refs, moves):
        ref[...] = all_ref[lax.rem(y_ref[0] + d, ways)].astype(ref.dtype)


def fold_b(y_index, parts, moves):
    ys, rows, width = parts[0].shape
    return pl.pallas_call(
        lambda *r: fold_b_body(*r, count=len(parts), moves=moves),
        in_specs=[SMEM] + [VMEM] * len(parts),
        out_specs=[VMEM] * len(moves),
        out_shape=[jax.ShapeDtypeStruct((rows, width), F32 if d == 0 else BF16) for d in moves],
        scratch_shapes=[pltpu.VMEM((ys, rows, width), F32)],
        compiler_params=PARAMS,
        cost_estimate=LONG,
    )(y_index, *parts)


def finish_body(odd_ref, *refs, count):
    out_ref = refs[-1]
    odd = odd_ref[0]
    for group, even_at, odd_at in ((refs[:count], 0, BLOCK // 2), (refs[count:-1], BLOCK, 0)):
        total = total_of([r[...] for r in group])
        at = pl.multiple_of(jnp.where(odd == 1, odd_at, even_at), BLOCK // 2)
        out_ref[pl.ds(at, total.shape[0])] = total


def finish(odd, first, second):
    width = first[0].shape[1]
    rows = first[0].shape[0] + second[0].shape[0]
    return pl.pallas_call(
        lambda *r: finish_body(*r, count=len(first)),
        in_specs=[SMEM] + [VMEM] * (len(first) + len(second)),
        out_specs=VMEM,
        out_shape=jax.ShapeDtypeStruct((rows, width), F32),
        compiler_params=PARAMS,
        cost_estimate=FREE,
    )(odd, *first, *second)


def solution(mesh):
    groups, spread = mesh.shape["seq"], mesh.shape["fsdp"]
    ys, zs = 4, spread // 4
    chips = groups // 2
    y_groups = [[y * zs + z for y in range(ys)] for z in range(zs)]
    z_groups = [[y * zs + z for z in range(zs)] for y in range(ys)]

    def along_x(a, d):
        return lax.ppermute(a, "seq", [(i, (i + 2 * d) % groups) for i in range(groups)])

    def swap(a):
        return lax.ppermute(a, "seq", [(i, i ^ 1) for i in range(groups)])

    def along_z(a, d):
        return lax.ppermute(a, "fsdp", [(y * zs + z, y * zs + (z + d) % zs) for y in range(ys) for z in range(zs)])

    def along_y(a, d):
        return lax.ppermute(a, "fsdp", [(y * zs + z, (y + d) % ys * zs + z) for y in range(ys) for z in range(zs)])

    def after(a, *others):
        return lax.optimization_barrier((a, *others))[0]

    def shards(queries, attn_keys, attn_values, grad_out, out_weight):
        me = lax.axis_index("seq")
        f = lax.axis_index("fsdp")
        x, core, yi, zi = me // 2, me % 2, f // zs, f % zs
        near = [(x - d) % chips * 2 for d in (0, 1, -1, 2)]
        pos = jnp.stack([n + core for n in near] + [n + 1 - core for n in near]).astype(jnp.int32)
        y_index = yi.astype(jnp.int32).reshape(1)
        z_index = zi.astype(jnp.int32).reshape(1)

        packed = pack_heads(queries, attn_keys, attn_values, groups)
        heads = lax.all_to_all(packed, "seq", 0, 0, tiled=True)
        weight = lax.all_gather(out_weight.T, "fsdp", axis=0).reshape(ys, zs, *out_weight.shape[::-1])

        chunk_a, chunk_b = pack_grad(after(grad_out, packed))
        same_a = [chunk_a] + [along_x(chunk_a, d) for d in (1, -1, 2)]
        same_b = [chunk_b] + [along_x(after(chunk_b, same_a[i], heads), d) for i, d in ((1, 1), (2, -1), (3, 2))]

        att, lse = attend(heads)
        got_a = same_a + [swap(after(a, att)) for a in same_a]
        term_a = find_term_a(pos, got_a, att, ys)
        got_b = same_b + [swap(after(b, term_a)) for b in same_b]
        both_a = lax.all_to_all(term_a, "fsdp", 0, 0, tiled=True, axis_index_groups=y_groups)
        term_b = find_term_b(after(pos, term_a), z_index, got_b, att, ys, zs)
        dout = find_dout(after(pos, term_b[0]), got_a, got_b, weight)
        grads = attend_grad(heads, dout, att, lse)
        back = lax.all_to_all(grads, "seq", 0, 0, tiled=True)

        parts_b = [along_z(term_b[d], d) for d in (1, 7, 2, 6, 4)] + [along_z(after(term_b[d], grads), d) for d in (3, 5)]
        away_b = fold_b(y_index, [term_b[0]] + parts_b, (0, 1, 3, 2))
        sums_b = [away_b[0]] + [along_y(b, d) for b, d in zip(away_b[1:], (1, -1, 2))]
        away_a = fold_a(z_index, after(both_a, grads), zs)
        sums_a = [away_a[0]] + [along_z(away_a[d], d) for d in range(1, zs)]
        grad_q, grad_k, grad_v = unpack_heads(back)
        grad_weight = finish(z_index % 2, sums_a, sums_b).T
        return grad_q, grad_k, grad_v, grad_weight

    tokens, weights = P("fsdp", "seq", None), P("seq", "fsdp")
    return jax.shard_map(
        shards,
        mesh=mesh,
        in_specs=(tokens, tokens, tokens, tokens, weights),
        out_specs=(tokens, tokens, tokens, weights),
        check_vma=False,
    )
```

```python
import math

import jax
import jax.numpy as jnp
from jax import lax
from jax.experimental import pallas as pl
from jax.experimental.pallas import tpu as pltpu
from jax.sharding import PartitionSpec as P

HEAD_DIM = 128
BLOCK = 128
F32 = jnp.float32
BF16 = jnp.bfloat16
NT = (((1,), (1,)), ((), ()))
PARAMS = pltpu.CompilerParams(vmem_limit_bytes=16 * 1024 * 1024)
FREE = pl.CostEstimate(flops=0, transcendentals=0, bytes_accessed=0)
LONG = pl.CostEstimate(flops=10**11, transcendentals=0, bytes_accessed=10**8)
ANY = pl.BlockSpec(memory_space=pl.ANY)
VMEM = pl.BlockSpec(memory_space=pltpu.VMEM)
SMEM = pl.BlockSpec(memory_space=pltpu.SMEM)


def dot(a, b):
    return jnp.dot(a, b, preferred_element_type=F32)


def dot_nt(a, b):
    return lax.dot_general(a, b, NT, preferred_element_type=F32)


def run_copies(pairs, sems):
    copies = [pltpu.make_async_copy(src, dst, sems.at[i]) for i, (src, dst) in enumerate(pairs)]
    for c in copies:
        c.start()
    for c in copies:
        c.wait()


def pack_heads_body(q_ref, k_ref, v_ref, out_ref, sems):
    groups, _, _, width = out_ref.shape
    run_copies(
        [
            (ref.at[0, :, i * width : (i + 1) * width], out_ref.at[i, j])
            for i in range(groups)
            for j, ref in enumerate((q_ref, k_ref, v_ref))
        ],
        sems,
    )


def pack_heads(q, k, v, groups):
    tokens, width = q.shape[1], q.shape[2] // groups
    return pl.pallas_call(
        pack_heads_body,
        in_specs=[VMEM] * 3,
        out_specs=ANY,
        out_shape=jax.ShapeDtypeStruct((groups, 3, tokens, width), BF16),
        scratch_shapes=[pltpu.SemaphoreType.DMA((3 * groups,))],
        compiler_params=PARAMS,
        cost_estimate=FREE,
    )(q, k, v)


def unpack_heads_body(x_ref, q_ref, k_ref, v_ref, sems):
    groups, _, _, width = x_ref.shape
    run_copies(
        [
            (x_ref.at[i, j], ref.at[0, :, i * width : (i + 1) * width])
            for i in range(groups)
            for j, ref in enumerate((q_ref, k_ref, v_ref))
        ],
        sems,
    )


def unpack_heads(x):
    groups, _, tokens, width = x.shape
    return pl.pallas_call(
        unpack_heads_body,
        in_specs=[VMEM],
        out_specs=[ANY] * 3,
        out_shape=[jax.ShapeDtypeStruct((1, tokens, groups * width), BF16)] * 3,
        scratch_shapes=[pltpu.SemaphoreType.DMA((3 * groups,))],
        compiler_params=PARAMS,
        cost_estimate=FREE,
    )(x)


def pack_grad_body(g_ref, a_ref, b_ref, sems):
    def cols(ref, at):
        return ref.at[:, at * BLOCK : (at + 1) * BLOCK]

    pairs = []
    for t in range(g_ref.shape[2] // (3 * BLOCK)):
        pairs += [
            (cols(g_ref.at[0], 3 * t), cols(a_ref, 2 * t)),
            (cols(g_ref.at[0], 3 * t + 2), cols(a_ref, 2 * t + 1)),
            (cols(g_ref.at[0], 3 * t + 1), cols(b_ref, t)),
        ]
    run_copies(pairs, sems)


def pack_grad(g):
    tokens, width = g.shape[1:]
    return pl.pallas_call(
        pack_grad_body,
        in_specs=[VMEM],
        out_specs=[ANY] * 2,
        out_shape=[
            jax.ShapeDtypeStruct((tokens, 2 * width // 3), BF16),
            jax.ShapeDtypeStruct((tokens, width // 3), BF16),
        ],
        scratch_shapes=[pltpu.SemaphoreType.DMA((width // BLOCK,))],
        compiler_params=PARAMS,
        cost_estimate=FREE,
    )(g)


def attend_body(x_ref, att_ref, lse_ref, *, step):
    groups, _, tokens, width = x_ref.shape
    length, dim = groups * tokens, HEAD_DIM
    fold = math.log2(math.e) / dim**0.5
    for h in range(width // dim):
        own = slice(h * dim, (h + 1) * dim)
        q = x_ref[:, 0, :, own].reshape(length, dim)
        k = x_ref[:, 1, :, own].reshape(length, dim)
        vt = x_ref[:, 2, :, own].reshape(length, dim).T
        for lo in range(0, length, step):
            s = dot_nt(k, q[lo : lo + step])
            top = jnp.max(s, axis=0, keepdims=True) * fold
            e = jnp.exp2(s * fold - top)
            total = jnp.sum(e, axis=0, keepdims=True)
            att_ref[own, lo : lo + step] = (dot(vt, e.astype(BF16)) * (1.0 / total)).astype(BF16)
            lse_ref[h, :, lo : lo + step] = top + jnp.log2(total)


def attend(x):
    groups, _, tokens, width = x.shape
    heads, length = width // HEAD_DIM, groups * tokens
    return pl.pallas_call(
        lambda *r: attend_body(*r, step=256),
        in_specs=[VMEM],
        out_specs=[VMEM] * 2,
        out_shape=[
            jax.ShapeDtypeStruct((width, length), BF16),
            jax.ShapeDtypeStruct((heads, 1, length), F32),
        ],
        compiler_params=PARAMS,
        cost_estimate=FREE,
    )(x)


def attend_grad_body(x_ref, do_ref, att_ref, lse_ref, out_ref, dk_ref, dv_ref, *, step):
    groups, _, tokens, width = x_ref.shape
    length, dim = groups * tokens, HEAD_DIM
    scale = 1.0 / dim**0.5
    fold = math.log2(math.e) * scale
    for h in range(width // dim):
        own = slice(h * dim, (h + 1) * dim)
        q = x_ref[:, 0, :, own].reshape(length, dim)
        k = x_ref[:, 1, :, own].reshape(length, dim)
        v = x_ref[:, 2, :, own].reshape(length, dim)
        kt = k.T
        for lo in range(0, length, step):
            qb = q[lo : lo + step]
            do = do_ref[lo : lo + step, own]
            p = jnp.exp2(dot_nt(k, qb) * fold - lse_ref[h, :, lo : lo + step])
            gp = dot_nt(v, do)
            do_t = do.astype(F32).T
            delta = jnp.sum(do_t * att_ref[own, lo : lo + step].astype(F32), axis=0, keepdims=True)
            gs = (p * (gp - delta)).astype(BF16)
            dv = dot(p.astype(BF16), do)
            dk = dot(gs, qb)
            if lo == 0:
                dv_ref[...] = dv
                dk_ref[...] = dk
            else:
                dv_ref[...] += dv
                dk_ref[...] += dk
            dq = (dot(kt, gs) * scale).T.astype(BF16)
            for j in range(step // tokens):
                out_ref[lo // tokens + j, 0, :, own] = dq[j * tokens : (j + 1) * tokens]
        out_ref[:, 1, :, own] = (dk_ref[...] * scale).astype(BF16).reshape(groups, tokens, dim)
        out_ref[:, 2, :, own] = dv_ref[...].astype(BF16).reshape(groups, tokens, dim)


def attend_grad(x, dout, att, lse):
    groups, _, tokens, _ = x.shape
    return pl.pallas_call(
        lambda *r: attend_grad_body(*r, step=256),
        in_specs=[VMEM] * 4,
        out_specs=VMEM,
        out_shape=jax.ShapeDtypeStruct(x.shape, BF16),
        scratch_shapes=[pltpu.VMEM((groups * tokens, HEAD_DIM), F32)] * 2,
        compiler_params=PARAMS,
        cost_estimate=FREE,
    )(x, dout, att, lse)


def chunk_rows(w_ref, y, first):
    parts = []
    for z in range(0, w_ref.shape[1], 2):
        if first:
            parts += [w_ref[y, z, :BLOCK], w_ref[y, z + 1, BLOCK // 2 :]]
        else:
            parts += [w_ref[y, z, BLOCK:], w_ref[y, z + 1, : BLOCK // 2]]
    return jnp.concatenate(parts, axis=0)


def dout_body(*refs, pieces):
    pos_ref, w_ref, out_ref, acc_ref = refs[0], refs[-3], refs[-2], refs[-1]
    a_refs, b_refs = refs[1 : 1 + pieces], refs[1 + pieces : 1 + 2 * pieces]
    tokens = a_refs[0].shape[0]
    ys = w_ref.shape[0]
    for y in range(ys):
        part = None
        for g_refs, first in ((a_refs, True), (b_refs, False)):
            step = g_refs[0].shape[1] // ys
            rows = jnp.concatenate([g[:, y * step : (y + 1) * step] for g in g_refs], axis=0)
            more = dot(rows, chunk_rows(w_ref, y, first))
            part = more if part is None else part + more
        if y == 0:
            acc_ref[...] = part
        elif y < ys - 1:
            acc_ref[...] += part
        else:
            for p in range(part.shape[0] // tokens):
                own = slice(p * tokens, (p + 1) * tokens)
                at = pl.ds(pl.multiple_of(pos_ref[p] * tokens, tokens), tokens)
                out_ref[at] = (acc_ref[own] + part[own]).astype(BF16)


def find_dout(pos, got_a, got_b, w):
    shape = (sum(g.shape[0] for g in got_a), w.shape[3])
    return pl.pallas_call(
        lambda *r: dout_body(*r, pieces=len(got_a)),
        in_specs=[SMEM] + [VMEM] * (2 * len(got_a) + 1),
        out_specs=VMEM,
        out_shape=jax.ShapeDtypeStruct(shape, BF16),
        scratch_shapes=[pltpu.VMEM(shape, F32)],
        compiler_params=PARAMS,
        cost_estimate=LONG,
    )(pos, *got_a, *got_b, w)


def own_order(pos_ref, att_ref, own_ref, tokens):
    for p in range(att_ref.shape[1] // tokens):
        at = pl.ds(pl.multiple_of(pos_ref[p] * tokens, tokens), tokens)
        own_ref[:, p * tokens : (p + 1) * tokens] = att_ref[:, at]


def term_a_body(*refs, pieces, step):
    pos_ref, g_refs, att_ref = refs[0], refs[1 : 1 + pieces], refs[1 + pieces]
    out_ref, own_ref = refs[-2:]
    ys, _, cols = out_ref.shape
    own_order(pos_ref, att_ref, own_ref, g_refs[0].shape[0])
    for y in range(ys):
        for lo in range(0, cols, step):
            at = y * cols + lo
            rows = jnp.concatenate([g[:, at : at + step] for g in g_refs], axis=0)
            out_ref[y, :, lo : lo + step] = dot(own_ref[...], rows).astype(BF16)


def find_term_a(pos, g, att, ys):
    cols = g[0].shape[1]
    width = att.shape[0]
    return pl.pallas_call(
        lambda *r: term_a_body(*r, pieces=len(g), step=512),
        in_specs=[SMEM] + [VMEM] * (len(g) + 1),
        out_specs=VMEM,
        out_shape=jax.ShapeDtypeStruct((ys, width, cols // ys), BF16),
        scratch_shapes=[pltpu.VMEM(att.shape, BF16)],
        compiler_params=PARAMS,
        cost_estimate=FREE,
    )(pos, *g, att)


def term_b_body(*refs, pieces, ways):
    pos_ref, z_ref, g_refs, att_ref = refs[0], refs[1], refs[2 : 2 + pieces], refs[2 + pieces]
    out_refs, own_ref, all_ref = refs[-2 - ways : -2], refs[-2], refs[-1]
    _, ys, rows_each, _ = all_ref.shape
    step = ways * rows_each
    own_order(pos_ref, att_ref, own_ref, g_refs[0].shape[0])
    for y in range(ys):
        rows = jnp.concatenate([g[:, y * step : (y + 1) * step] for g in g_refs], axis=0)
        flat = dot(own_ref[...], rows).T.astype(BF16)
        for z in range(ways):
            all_ref[z, y] = flat[z * rows_each : (z + 1) * rows_each]
    for d in range(ways):
        out_refs[d][...] = all_ref[lax.rem(z_ref[0] + d, ways)]


def find_term_b(pos, z_index, g, att, ys, zs):
    cols = g[0].shape[1]
    width = att.shape[0]
    piece = (ys, cols // ys // zs, width)
    return pl.pallas_call(
        lambda *r: term_b_body(*r, pieces=len(g), ways=zs),
        in_specs=[SMEM] * 2 + [VMEM] * (len(g) + 1),
        out_specs=[VMEM] * zs,
        out_shape=[jax.ShapeDtypeStruct(piece, BF16)] * zs,
        scratch_shapes=[pltpu.VMEM(att.shape, BF16), pltpu.VMEM((zs, *piece), BF16)],
        compiler_params=PARAMS,
        cost_estimate=FREE,
    )(pos, z_index, *g, att)


def total_of(values):
    total = values[0].astype(F32)
    for v in values[1:]:
        total = total + v.astype(F32)
    return total


def fold_a_body(z_ref, x_ref, *refs):
    out_refs, all_ref = refs[:-1], refs[-1]
    ways = len(out_refs)
    step = x_ref.shape[2] // ways
    for z in range(ways):
        own = slice(z * step, (z + 1) * step)
        all_ref[z] = total_of([x_ref[i, :, own] for i in range(x_ref.shape[0])]).T.astype(BF16)
    for d in range(ways):
        out_refs[d][...] = all_ref[lax.rem(z_ref[0] + d, ways)]


def fold_a(z_index, x, ways):
    _, width, cols = x.shape
    piece = (cols // ways, width)
    return pl.pallas_call(
        fold_a_body,
        in_specs=[SMEM, VMEM],
        out_specs=[VMEM] * ways,
        out_shape=[jax.ShapeDtypeStruct(piece, BF16)] * ways,
        scratch_shapes=[pltpu.VMEM((ways, *piece), BF16)],
        compiler_params=PARAMS,
        cost_estimate=LONG,
    )(z_index, x)


def fold_b_body(y_ref, *refs, count, moves):
    in_refs, out_refs, all_ref = refs[:count], refs[count:-1], refs[-1]
    ways = all_ref.shape[0]
    for y in range(ways):
        all_ref[y] = total_of([r[y] for r in in_refs])
    for ref, d in zip(out_refs, moves):
        ref[...] = all_ref[lax.rem(y_ref[0] + d, ways)].astype(ref.dtype)


def fold_b(y_index, parts, moves):
    ys, rows, width = parts[0].shape
    return pl.pallas_call(
        lambda *r: fold_b_body(*r, count=len(parts), moves=moves),
        in_specs=[SMEM] + [VMEM] * len(parts),
        out_specs=[VMEM] * len(moves),
        out_shape=[jax.ShapeDtypeStruct((rows, width), F32 if d == 0 else BF16) for d in moves],
        scratch_shapes=[pltpu.VMEM((ys, rows, width), F32)],
        compiler_params=PARAMS,
        cost_estimate=LONG,
    )(y_index, *parts)


def finish_body(odd_ref, *refs, count):
    out_ref = refs[-1]
    odd = odd_ref[0]
    for group, even_at, odd_at in ((refs[:count], 0, BLOCK // 2), (refs[count:-1], BLOCK, 0)):
        total = total_of([r[...] for r in group])
        at = pl.multiple_of(jnp.where(odd == 1, odd_at, even_at), BLOCK // 2)
        out_ref[pl.ds(at, total.shape[0])] = total


def finish(odd, first, second):
    width = first[0].shape[1]
    rows = first[0].shape[0] + second[0].shape[0]
    return pl.pallas_call(
        lambda *r: finish_body(*r, count=len(first)),
        in_specs=[SMEM] + [VMEM] * (len(first) + len(second)),
        out_specs=VMEM,
        out_shape=jax.ShapeDtypeStruct((rows, width), F32),
        compiler_params=PARAMS,
        cost_estimate=FREE,
    )(odd, *first, *second)


def solution(mesh):
    groups, spread = mesh.shape["seq"], mesh.shape["fsdp"]
    ys, zs = 4, spread // 4
    chips = groups // 2
    y_groups = [[y * zs + z for y in range(ys)] for z in range(zs)]
    z_groups = [[y * zs + z for z in range(zs)] for y in range(ys)]

    def along_x(a, d):
        return lax.ppermute(a, "seq", [(i, (i + 2 * d) % groups) for i in range(groups)])

    def swap(a):
        return lax.ppermute(a, "seq", [(i, i ^ 1) for i in range(groups)])

    def along_z(a, d):
        return lax.ppermute(a, "fsdp", [(y * zs + z, y * zs + (z + d) % zs) for y in range(ys) for z in range(zs)])

    def along_y(a, d):
        return lax.ppermute(a, "fsdp", [(y * zs + z, (y + d) % ys * zs + z) for y in range(ys) for z in range(zs)])

    def after(a, *others):
        return lax.optimization_barrier((a, *others))[0]

    def shards(queries, attn_keys, attn_values, grad_out, out_weight):
        me = lax.axis_index("seq")
        f = lax.axis_index("fsdp")
        x, core, yi, zi = me // 2, me % 2, f // zs, f % zs
        near = [(x - d) % chips * 2 for d in (0, 1, -1, 2)]
        pos = jnp.stack([n + core for n in near] + [n + 1 - core for n in near]).astype(jnp.int32)
        y_index = yi.astype(jnp.int32).reshape(1)
        z_index = zi.astype(jnp.int32).reshape(1)

        packed = pack_heads(queries, attn_keys, attn_values, groups)
        heads = lax.all_to_all(packed, "seq", 0, 0, tiled=True)
        weight = lax.all_gather(out_weight.T, "fsdp", axis=0).reshape(ys, zs, *out_weight.shape[::-1])

        chunk_a, chunk_b = pack_grad(after(grad_out, packed))
        half = chunk_a.shape[0] // 2
        left_a, right_a = along_x(chunk_a, 1), along_x(chunk_a, -1)
        att, lse = attend(heads)
        far_a = [along_x(after(left_a[:half], att), 1), along_x(after(right_a[half:], att), -1)]
        same_a = [chunk_a, left_a, right_a, *far_a]
        got_a = same_a + [swap(after(a, att)) for a in same_a]

        left_b, right_b = along_x(after(chunk_b, far_a[0]), 1), along_x(after(chunk_b, far_a[1]), -1)
        term_a = find_term_a(pos, got_a, att, ys)
        far_b = [along_x(after(left_b[:half], term_a), 1), along_x(after(right_b[half:], term_a), -1)]
        same_b = [chunk_b, left_b, right_b, *far_b]
        got_b = same_b + [swap(after(b, term_a)) for b in same_b]
        both_a = lax.all_to_all(term_a, "fsdp", 0, 0, tiled=True, axis_index_groups=y_groups)
        term_b = find_term_b(after(pos, term_a), z_index, got_b, att, ys, zs)
        dout = find_dout(after(pos, term_b[0]), got_a, got_b, weight)
        grads = attend_grad(heads, dout, att, lse)
        back = lax.all_to_all(grads, "seq", 0, 0, tiled=True)

        parts_b = [along_z(term_b[d], d) for d in (1, 7, 2, 6, 4)] + [along_z(after(term_b[d], grads), d) for d in (3, 5)]
        away_b = fold_b(y_index, [term_b[0]] + parts_b, (0, 1, 3, 2))
        sums_b = [away_b[0]] + [along_y(b, d) for b, d in zip(away_b[1:], (1, -1, 2))]
        away_a = fold_a(z_index, after(both_a, grads), zs)
        sums_a = [away_a[0]] + [along_z(away_a[d], d) for d in range(1, zs)]
        grad_q, grad_k, grad_v = unpack_heads(back)
        grad_weight = finish(z_index % 2, sums_a, sums_b).T
        return grad_q, grad_k, grad_v, grad_weight

    tokens, weights = P("fsdp", "seq", None), P("seq", "fsdp")
    return jax.shard_map(
        shards,
        mesh=mesh,
        in_specs=(tokens, tokens, tokens, tokens, weights),
        out_specs=(tokens, tokens, tokens, weights),
        check_vma=False,
    )
```

```python
import math

import jax
import jax.numpy as jnp
from jax import lax
from jax.experimental import pallas as pl
from jax.experimental.pallas import tpu as pltpu
from jax.sharding import PartitionSpec as P

HEAD_DIM = 128
BLOCK = 128
F32 = jnp.float32
BF16 = jnp.bfloat16
NT = (((1,), (1,)), ((), ()))
PARAMS = pltpu.CompilerParams(vmem_limit_bytes=12 * 1024 * 1024)
FREE = pl.CostEstimate(flops=0, transcendentals=0, bytes_accessed=0)
HUGE = pl.CostEstimate(flops=10**13, transcendentals=0, bytes_accessed=10**8)
MID = pl.CostEstimate(flops=2 * 10**10, transcendentals=0, bytes_accessed=10**6)
LONG = pl.CostEstimate(flops=10**11, transcendentals=0, bytes_accessed=10**8)
ANY = pl.BlockSpec(memory_space=pl.ANY)
VMEM = pl.BlockSpec(memory_space=pltpu.VMEM)
SMEM = pl.BlockSpec(memory_space=pltpu.SMEM)


def dot(a, b):
    return jnp.dot(a, b, preferred_element_type=F32)


def dot_nt(a, b):
    return lax.dot_general(a, b, NT, preferred_element_type=F32)


def run_copies(pairs, sems):
    copies = [pltpu.make_async_copy(src, dst, sems.at[i]) for i, (src, dst) in enumerate(pairs)]
    for c in copies:
        c.start()
    for c in copies:
        c.wait()


def pack_heads_body(q_ref, k_ref, v_ref, out_ref, sems):
    groups, _, _, width = out_ref.shape
    run_copies(
        [
            (ref.at[0, :, i * width : (i + 1) * width], out_ref.at[i, j])
            for i in range(groups)
            for j, ref in enumerate((q_ref, k_ref, v_ref))
        ],
        sems,
    )


def pack_heads(q, k, v, groups):
    tokens, width = q.shape[1], q.shape[2] // groups
    return pl.pallas_call(
        pack_heads_body,
        in_specs=[VMEM] * 3,
        out_specs=ANY,
        out_shape=jax.ShapeDtypeStruct((groups, 3, tokens, width), BF16),
        scratch_shapes=[pltpu.SemaphoreType.DMA((3 * groups,))],
        compiler_params=PARAMS,
        cost_estimate=FREE,
    )(q, k, v)


def unpack_heads_body(x_ref, q_ref, k_ref, v_ref, sems):
    groups, _, _, width = x_ref.shape
    run_copies(
        [
            (x_ref.at[i, j], ref.at[0, :, i * width : (i + 1) * width])
            for i in range(groups)
            for j, ref in enumerate((q_ref, k_ref, v_ref))
        ],
        sems,
    )


def unpack_heads(x):
    groups, _, tokens, width = x.shape
    return pl.pallas_call(
        unpack_heads_body,
        in_specs=[VMEM],
        out_specs=[ANY] * 3,
        out_shape=[jax.ShapeDtypeStruct((1, tokens, groups * width), BF16)] * 3,
        scratch_shapes=[pltpu.SemaphoreType.DMA((3 * groups,))],
        compiler_params=PARAMS,
        cost_estimate=FREE,
    )(x)


def pack_grad_body(g_ref, a_ref, b_ref, sems):
    def cols(ref, at):
        return ref.at[:, at * BLOCK : (at + 1) * BLOCK]

    pairs = []
    for t in range(g_ref.shape[2] // (3 * BLOCK)):
        pairs += [
            (cols(g_ref.at[0], 3 * t), cols(a_ref, 2 * t)),
            (cols(g_ref.at[0], 3 * t + 2), cols(a_ref, 2 * t + 1)),
            (cols(g_ref.at[0], 3 * t + 1), cols(b_ref, t)),
        ]
    run_copies(pairs, sems)


def pack_grad(g):
    tokens, width = g.shape[1:]
    return pl.pallas_call(
        pack_grad_body,
        in_specs=[VMEM],
        out_specs=[ANY] * 2,
        out_shape=[
            jax.ShapeDtypeStruct((tokens, 2 * width // 3), BF16),
            jax.ShapeDtypeStruct((tokens, width // 3), BF16),
        ],
        scratch_shapes=[pltpu.SemaphoreType.DMA((width // BLOCK,))],
        compiler_params=PARAMS,
        cost_estimate=FREE,
    )(g)


def attend_body(x_ref, att_ref, lse_ref, *, step):
    groups, _, tokens, width = x_ref.shape
    length, dim = groups * tokens, HEAD_DIM
    fold = math.log2(math.e) / dim**0.5
    for h in range(width // dim):
        own = slice(h * dim, (h + 1) * dim)
        q = x_ref[:, 0, :, own].reshape(length, dim)
        k = x_ref[:, 1, :, own].reshape(length, dim)
        vt = x_ref[:, 2, :, own].reshape(length, dim).T
        for lo in range(0, length, step):
            s = dot_nt(k, q[lo : lo + step])
            top = jnp.max(s, axis=0, keepdims=True) * fold
            e = jnp.exp2(s * fold - top)
            total = jnp.sum(e, axis=0, keepdims=True)
            att_ref[own, lo : lo + step] = (dot(vt, e.astype(BF16)) * (1.0 / total)).astype(BF16)
            lse_ref[h, :, lo : lo + step] = top + jnp.log2(total)


def attend(x):
    groups, _, tokens, width = x.shape
    heads, length = width // HEAD_DIM, groups * tokens
    return pl.pallas_call(
        lambda *r: attend_body(*r, step=256),
        in_specs=[VMEM],
        out_specs=[VMEM] * 2,
        out_shape=[
            jax.ShapeDtypeStruct((width, length), BF16),
            jax.ShapeDtypeStruct((heads, 1, length), F32),
        ],
        compiler_params=PARAMS,
        cost_estimate=FREE,
    )(x)


def attend_grad_body(x_ref, do_ref, att_ref, lse_ref, out_ref, dk_ref, dv_ref, *, step):
    groups, _, tokens, width = x_ref.shape
    length, dim = groups * tokens, HEAD_DIM
    scale = 1.0 / dim**0.5
    fold = math.log2(math.e) * scale
    for h in range(width // dim):
        own = slice(h * dim, (h + 1) * dim)
        q = x_ref[:, 0, :, own].reshape(length, dim)
        k = x_ref[:, 1, :, own].reshape(length, dim)
        v = x_ref[:, 2, :, own].reshape(length, dim)
        kt = k.T
        for lo in range(0, length, step):
            qb = q[lo : lo + step]
            do = do_ref[lo : lo + step, own]
            p = jnp.exp2(dot_nt(k, qb) * fold - lse_ref[h, :, lo : lo + step])
            gp = dot_nt(v, do)
            do_t = do.astype(F32).T
            delta = jnp.sum(do_t * att_ref[own, lo : lo + step].astype(F32), axis=0, keepdims=True)
            gs = (p * (gp - delta)).astype(BF16)
            dv = dot(p.astype(BF16), do)
            dk = dot(gs, qb)
            if lo == 0:
                dv_ref[...] = dv
                dk_ref[...] = dk
            else:
                dv_ref[...] += dv
                dk_ref[...] += dk
            dq = (dot(kt, gs) * scale).T.astype(BF16)
            for j in range(step // tokens):
                out_ref[lo // tokens + j, 0, :, own] = dq[j * tokens : (j + 1) * tokens]
        out_ref[:, 1, :, own] = (dk_ref[...] * scale).astype(BF16).reshape(groups, tokens, dim)
        out_ref[:, 2, :, own] = dv_ref[...].astype(BF16).reshape(groups, tokens, dim)


def attend_grad(x, dout, att, lse):
    groups, _, tokens, _ = x.shape
    return pl.pallas_call(
        lambda *r: attend_grad_body(*r, step=256),
        in_specs=[VMEM] * 4,
        out_specs=VMEM,
        out_shape=jax.ShapeDtypeStruct(x.shape, BF16),
        scratch_shapes=[pltpu.VMEM((groups * tokens, HEAD_DIM), F32)] * 2,
        compiler_params=PARAMS,
        cost_estimate=FREE,
    )(x, dout, att, lse)


def chunk_rows(w_ref, y, first):
    parts = []
    for z in range(0, w_ref.shape[1], 2):
        if first:
            parts += [w_ref[y, z, :BLOCK], w_ref[y, z + 1, BLOCK // 2 :]]
        else:
            parts += [w_ref[y, z, BLOCK:], w_ref[y, z + 1, : BLOCK // 2]]
    return jnp.concatenate(parts, axis=0)


def dout_a_body(*refs):
    g_refs, w_ref, out_ref = refs[:-2], refs[-2], refs[-1]
    ys = w_ref.shape[0]
    step = g_refs[0].shape[1] // ys
    for y in range(ys):
        rows = jnp.concatenate([g[:, y * step : (y + 1) * step] for g in g_refs], axis=0)
        part = dot(rows, chunk_rows(w_ref, y, True))
        if y == 0:
            out_ref[...] = part
        else:
            out_ref[...] += part


def find_dout_a(got, w):
    return pl.pallas_call(
        dout_a_body,
        in_specs=[VMEM] * (len(got) + 1),
        out_specs=VMEM,
        out_shape=jax.ShapeDtypeStruct((sum(g.shape[0] for g in got), w.shape[3]), F32),
        compiler_params=PARAMS,
        cost_estimate=FREE,
    )(*got, w)


def dout_b_body(*refs):
    pos_ref, g_refs, w_ref, base_ref, out_ref, acc_ref = refs[0], refs[1:-4], *refs[-4:]
    tokens, cols = g_refs[0].shape
    ys = w_ref.shape[0]
    step = cols // ys
    for y in range(ys):
        rows = jnp.concatenate([g[:, y * step : (y + 1) * step] for g in g_refs], axis=0)
        part = dot(rows, chunk_rows(w_ref, y, False))
        if y == 0:
            acc_ref[...] = base_ref[...] + part
        elif y < ys - 1:
            acc_ref[...] += part
        else:
            for p in range(part.shape[0] // tokens):
                own = slice(p * tokens, (p + 1) * tokens)
                at = pl.ds(pl.multiple_of(pos_ref[p] * tokens, tokens), tokens)
                out_ref[at] = (acc_ref[own] + part[own]).astype(BF16)


def find_dout_b(pos, got, w, base):
    return pl.pallas_call(
        dout_b_body,
        in_specs=[SMEM] + [VMEM] * (len(got) + 2),
        out_specs=VMEM,
        out_shape=jax.ShapeDtypeStruct(base.shape, BF16),
        scratch_shapes=[pltpu.VMEM(base.shape, F32)],
        compiler_params=PARAMS,
        cost_estimate=FREE,
    )(pos, *got, w, base)


def own_order(pos_ref, att_ref, own_ref, tokens):
    for p in range(att_ref.shape[1] // tokens):
        at = pl.ds(pl.multiple_of(pos_ref[p] * tokens, tokens), tokens)
        own_ref[:, p * tokens : (p + 1) * tokens] = att_ref[:, at]


def term_a_body(*refs, pieces, step, moves):
    pos_ref, y_ref, g_refs, att_ref = refs[0], refs[1], refs[2 : 2 + pieces], refs[2 + pieces]
    out_refs, own_ref = refs[3 + pieces : -1], refs[-1]
    ways, cols = len(out_refs), out_refs[0].shape[1]
    own_order(pos_ref, att_ref, own_ref, g_refs[0].shape[0])
    for out_ref, d in zip(out_refs, moves):
        base = lax.rem(y_ref[0] + d, ways) * cols
        for lo in range(0, cols, step):
            at = pl.ds(pl.multiple_of(base + lo, step), step)
            rows = jnp.concatenate([g[:, at] for g in g_refs], axis=0)
            out_ref[:, lo : lo + step] = dot(own_ref[...], rows).astype(BF16)


def find_term_a(pos, y_index, g, att, moves):
    shape = (att.shape[0], g[0].shape[1] // len(moves))
    return pl.pallas_call(
        lambda *r: term_a_body(*r, pieces=len(g), step=512, moves=moves),
        in_specs=[SMEM] * 2 + [VMEM] * (len(g) + 1),
        out_specs=[VMEM] * len(moves),
        out_shape=[jax.ShapeDtypeStruct(shape, BF16)] * len(moves),
        scratch_shapes=[pltpu.VMEM(att.shape, BF16)],
        compiler_params=PARAMS,
        cost_estimate=FREE,
    )(pos, y_index, *g, att)


def term_b_body(*refs, pieces, ways):
    pos_ref, z_ref, g_refs, att_ref = refs[0], refs[1], refs[2 : 2 + pieces], refs[2 + pieces]
    out_refs, own_ref, all_ref = refs[-2 - ways : -2], refs[-2], refs[-1]
    _, ys, rows_each, _ = all_ref.shape
    step = ways * rows_each
    own_order(pos_ref, att_ref, own_ref, g_refs[0].shape[0])
    for y in range(ys):
        rows = jnp.concatenate([g[:, y * step : (y + 1) * step] for g in g_refs], axis=0)
        flat = dot(own_ref[...], rows).T.astype(BF16)
        for z in range(ways):
            all_ref[z, y] = flat[z * rows_each : (z + 1) * rows_each]
    for d in range(ways):
        out_refs[d][...] = all_ref[lax.rem(z_ref[0] + d, ways)]


def find_term_b(pos, z_index, g, att, ys, zs):
    cols = g[0].shape[1]
    width = att.shape[0]
    piece = (ys, cols // ys // zs, width)
    return pl.pallas_call(
        lambda *r: term_b_body(*r, pieces=len(g), ways=zs),
        in_specs=[SMEM] * 2 + [VMEM] * (len(g) + 1),
        out_specs=[VMEM] * zs,
        out_shape=[jax.ShapeDtypeStruct(piece, BF16)] * zs,
        scratch_shapes=[pltpu.VMEM(att.shape, BF16), pltpu.VMEM((zs, *piece), BF16)],
        compiler_params=PARAMS,
        cost_estimate=FREE,
    )(pos, z_index, *g, att)


def total_of(values):
    total = values[0].astype(F32)
    for v in values[1:]:
        total = total + v.astype(F32)
    return total


def fold_a_body(z_ref, *refs, count):
    x_refs, out_refs, all_ref = refs[:count], refs[count:-1], refs[-1]
    ways = len(out_refs)
    step = x_refs[0].shape[1] // ways
    for z in range(ways):
        own = slice(z * step, (z + 1) * step)
        all_ref[z] = total_of([x[:, own] for x in x_refs]).T.astype(BF16)
    for d in range(ways):
        out_refs[d][...] = all_ref[lax.rem(z_ref[0] + d, ways)]


def fold_a(z_index, parts, ways):
    width, cols = parts[0].shape
    piece = (cols // ways, width)
    return pl.pallas_call(
        lambda *r: fold_a_body(*r, count=len(parts)),
        in_specs=[SMEM] + [VMEM] * len(parts),
        out_specs=[VMEM] * ways,
        out_shape=[jax.ShapeDtypeStruct(piece, BF16)] * ways,
        scratch_shapes=[pltpu.VMEM((ways, *piece), BF16)],
        compiler_params=PARAMS,
        cost_estimate=LONG,
    )(z_index, *parts)


def fold_b_body(y_ref, *refs, count, moves):
    in_refs, out_refs, all_ref = refs[:count], refs[count:-1], refs[-1]
    ways = all_ref.shape[0]
    for y in range(ways):
        all_ref[y] = total_of([r[y] for r in in_refs])
    for ref, d in zip(out_refs, moves):
        ref[...] = all_ref[lax.rem(y_ref[0] + d, ways)].astype(ref.dtype)


def fold_b(y_index, parts, moves):
    ys, rows, width = parts[0].shape
    return pl.pallas_call(
        lambda *r: fold_b_body(*r, count=len(parts), moves=moves),
        in_specs=[SMEM] + [VMEM] * len(parts),
        out_specs=[VMEM] * len(moves),
        out_shape=[jax.ShapeDtypeStruct((rows, width), F32 if d == 0 else BF16) for d in moves],
        scratch_shapes=[pltpu.VMEM((ys, rows, width), F32)],
        compiler_params=PARAMS,
        cost_estimate=LONG,
    )(y_index, *parts)


def finish_body(odd_ref, *refs, count):
    out_ref = refs[-1]
    odd = odd_ref[0]
    for group, even_at, odd_at in ((refs[:count], 0, BLOCK // 2), (refs[count:-1], BLOCK, 0)):
        total = total_of([r[...] for r in group])
        at = pl.multiple_of(jnp.where(odd == 1, odd_at, even_at), BLOCK // 2)
        out_ref[pl.ds(at, total.shape[0])] = total


def finish(odd, first, second):
    width = first[0].shape[1]
    rows = first[0].shape[0] + second[0].shape[0]
    return pl.pallas_call(
        lambda *r: finish_body(*r, count=len(first)),
        in_specs=[SMEM] + [VMEM] * (len(first) + len(second)),
        out_specs=VMEM,
        out_shape=jax.ShapeDtypeStruct((rows, width), F32),
        compiler_params=PARAMS,
        cost_estimate=FREE,
    )(odd, *first, *second)


def solution(mesh):
    groups, spread = mesh.shape["seq"], mesh.shape["fsdp"]
    ys, zs = 4, spread // 4
    chips = groups // 2
    y_groups = [[y * zs + z for y in range(ys)] for z in range(zs)]
    z_groups = [[y * zs + z for z in range(zs)] for y in range(ys)]

    def along_x(a, d):
        return lax.ppermute(a, "seq", [(i, (i + 2 * d) % groups) for i in range(groups)])

    def swap(a):
        return lax.ppermute(a, "seq", [(i, i ^ 1) for i in range(groups)])

    def along_z(a, d):
        return lax.ppermute(a, "fsdp", [(y * zs + z, y * zs + (z + d) % zs) for y in range(ys) for z in range(zs)])

    def along_y(a, d):
        return lax.ppermute(a, "fsdp", [(y * zs + z, (y + d) % ys * zs + z) for y in range(ys) for z in range(zs)])

    def after(a, *others):
        return lax.optimization_barrier((a, *others))[0]

    def shards(queries, attn_keys, attn_values, grad_out, out_weight):
        me = lax.axis_index("seq")
        f = lax.axis_index("fsdp")
        x, core, yi, zi = me // 2, me % 2, f // zs, f % zs
        near = [(x - d) % chips * 2 for d in (0, 1, -1, 2)]
        pos = jnp.stack([n + core for n in near] + [n + 1 - core for n in near]).astype(jnp.int32)
        y_index = yi.astype(jnp.int32).reshape(1)
        z_index = zi.astype(jnp.int32).reshape(1)

        packed = pack_heads(queries, attn_keys, attn_values, groups)
        heads = lax.all_to_all(packed, "seq", 0, 0, tiled=True)
        weight = lax.all_gather(out_weight.T, "fsdp", axis=0).reshape(ys, zs, *out_weight.shape[::-1])

        chunk_a, chunk_b = pack_grad(after(grad_out, packed))
        half = chunk_a.shape[0] // 2
        left_a, right_a = along_x(chunk_a, 1), along_x(chunk_a, -1)
        att, lse = attend(heads)
        far_a = [along_x(after(left_a, att)[:half], 1), along_x(after(right_a, att)[half:], -1)]
        same_a = [chunk_a, left_a, right_a, *far_a]
        got_a = same_a + [swap(after(a, att)) for a in same_a]

        left_b, right_b = along_x(after(chunk_b, far_a[0]), 1), along_x(after(chunk_b, far_a[1]), -1)
        turns = (0, 1, ys - 1, 2)
        term_a = find_term_a(pos, y_index, got_a, att, turns)
        parts_a = [term_a[0]] + [along_y(a, d) for a, d in zip(term_a[1:], turns[1:])]
        far_b = [along_x(after(left_b, term_a[0])[:half], 1), along_x(after(right_b, term_a[0])[half:], -1)]
        same_b = [chunk_b, left_b, right_b, *far_b]
        got_b = same_b + [swap(after(b, term_a[0])) for b in same_b]
        term_b = find_term_b(after(pos, *parts_a[1:3]), z_index, got_b, att, ys, zs)
        part = find_dout_a(got_a, after(weight, term_a[0]))
        dout = find_dout_b(after(pos, term_b[0]), got_b, weight, part)
        grads = attend_grad(heads, after(dout, parts_a[3]), att, lse)
        back = lax.all_to_all(grads, "seq", 0, 0, tiled=True)

        parts_b = [along_z(term_b[d], d) for d in (1, 7, 2, 6, 4)] + [along_z(after(term_b[d], grads), d) for d in (3, 5)]
        away_b = fold_b(y_index, [term_b[0]] + parts_b, turns)
        sums_b = [away_b[0]] + [along_y(b, d) for b, d in zip(away_b[1:], turns[1:])]
        away_a = fold_a(z_index, [after(parts_a[0], grads)] + parts_a[1:], zs)
        sums_a = [away_a[0]] + [along_z(away_a[d], d) for d in range(1, zs)]
        grad_q, grad_k, grad_v = unpack_heads(back)
        grad_weight = finish(z_index % 2, sums_a, sums_b).T
        return grad_q, grad_k, grad_v, grad_weight

    tokens, weights = P("fsdp", "seq", None), P("seq", "fsdp")
    return jax.shard_map(
        shards,
        mesh=mesh,
        in_specs=(tokens, tokens, tokens, tokens, weights),
        out_specs=(tokens, tokens, tokens, weights),
        check_vma=False,
    )
```

```python
import math

import jax
import jax.numpy as jnp
from jax import lax
from jax.experimental import pallas as pl
from jax.experimental.pallas import tpu as pltpu
from jax.sharding import PartitionSpec as P

HEAD_DIM = 128
BLOCK = 128
F32 = jnp.float32
BF16 = jnp.bfloat16
NT = (((1,), (1,)), ((), ()))
PARAMS = pltpu.CompilerParams(vmem_limit_bytes=12 * 1024 * 1024)
FREE = pl.CostEstimate(flops=0, transcendentals=0, bytes_accessed=0)
HUGE = pl.CostEstimate(flops=10**13, transcendentals=0, bytes_accessed=10**8)
MID = pl.CostEstimate(flops=2 * 10**10, transcendentals=0, bytes_accessed=10**6)
LONG = pl.CostEstimate(flops=10**11, transcendentals=0, bytes_accessed=10**8)
ANY = pl.BlockSpec(memory_space=pl.ANY)
VMEM = pl.BlockSpec(memory_space=pltpu.VMEM)
SMEM = pl.BlockSpec(memory_space=pltpu.SMEM)


def dot(a, b):
    return jnp.dot(a, b, preferred_element_type=F32)


def dot_nt(a, b):
    return lax.dot_general(a, b, NT, preferred_element_type=F32)


def run_copies(pairs, sems):
    copies = [pltpu.make_async_copy(src, dst, sems.at[i]) for i, (src, dst) in enumerate(pairs)]
    for c in copies:
        c.start()
    for c in copies:
        c.wait()


def pack_heads_body(q_ref, k_ref, v_ref, out_ref, sems):
    groups, _, _, width = out_ref.shape
    run_copies(
        [
            (ref.at[0, :, i * width : (i + 1) * width], out_ref.at[i, j])
            for i in range(groups)
            for j, ref in enumerate((q_ref, k_ref, v_ref))
        ],
        sems,
    )


def pack_heads(q, k, v, groups):
    tokens, width = q.shape[1], q.shape[2] // groups
    return pl.pallas_call(
        pack_heads_body,
        in_specs=[VMEM] * 3,
        out_specs=ANY,
        out_shape=jax.ShapeDtypeStruct((groups, 3, tokens, width), BF16),
        scratch_shapes=[pltpu.SemaphoreType.DMA((3 * groups,))],
        compiler_params=PARAMS,
        cost_estimate=FREE,
    )(q, k, v)


def unpack_heads_body(x_ref, q_ref, k_ref, v_ref, sems):
    groups, _, _, width = x_ref.shape
    run_copies(
        [
            (x_ref.at[i, j], ref.at[0, :, i * width : (i + 1) * width])
            for i in range(groups)
            for j, ref in enumerate((q_ref, k_ref, v_ref))
        ],
        sems,
    )


def unpack_heads(x):
    groups, _, tokens, width = x.shape
    return pl.pallas_call(
        unpack_heads_body,
        in_specs=[VMEM],
        out_specs=[ANY] * 3,
        out_shape=[jax.ShapeDtypeStruct((1, tokens, groups * width), BF16)] * 3,
        scratch_shapes=[pltpu.SemaphoreType.DMA((3 * groups,))],
        compiler_params=PARAMS,
        cost_estimate=FREE,
    )(x)


def pack_grad_body(g_ref, a_ref, b_ref, sems):
    def cols(ref, at):
        return ref.at[:, at * BLOCK : (at + 1) * BLOCK]

    pairs = []
    for t in range(g_ref.shape[2] // (3 * BLOCK)):
        pairs += [
            (cols(g_ref.at[0], 3 * t), cols(a_ref, 2 * t)),
            (cols(g_ref.at[0], 3 * t + 2), cols(a_ref, 2 * t + 1)),
            (cols(g_ref.at[0], 3 * t + 1), cols(b_ref, t)),
        ]
    run_copies(pairs, sems)


def pack_grad(g):
    tokens, width = g.shape[1:]
    return pl.pallas_call(
        pack_grad_body,
        in_specs=[VMEM],
        out_specs=[ANY] * 2,
        out_shape=[
            jax.ShapeDtypeStruct((tokens, 2 * width // 3), BF16),
            jax.ShapeDtypeStruct((tokens, width // 3), BF16),
        ],
        scratch_shapes=[pltpu.SemaphoreType.DMA((width // BLOCK,))],
        compiler_params=PARAMS,
        cost_estimate=FREE,
    )(g)


def attend_body(x_ref, att_ref, lse_ref, *, step):
    groups, _, tokens, width = x_ref.shape
    length, dim = groups * tokens, HEAD_DIM
    fold = math.log2(math.e) / dim**0.5
    for h in range(width // dim):
        own = slice(h * dim, (h + 1) * dim)
        q = x_ref[:, 0, :, own].reshape(length, dim)
        k = x_ref[:, 1, :, own].reshape(length, dim)
        vt = x_ref[:, 2, :, own].reshape(length, dim).T
        for lo in range(0, length, step):
            s = dot_nt(k, q[lo : lo + step])
            top = jnp.max(s, axis=0, keepdims=True) * fold
            e = jnp.exp2(s * fold - top)
            total = jnp.sum(e, axis=0, keepdims=True)
            att_ref[own, lo : lo + step] = (dot(vt, e.astype(BF16)) * (1.0 / total)).astype(BF16)
            lse_ref[h, :, lo : lo + step] = top + jnp.log2(total)


def attend(x):
    groups, _, tokens, width = x.shape
    heads, length = width // HEAD_DIM, groups * tokens
    return pl.pallas_call(
        lambda *r: attend_body(*r, step=256),
        in_specs=[VMEM],
        out_specs=[VMEM] * 2,
        out_shape=[
            jax.ShapeDtypeStruct((width, length), BF16),
            jax.ShapeDtypeStruct((heads, 1, length), F32),
        ],
        compiler_params=PARAMS,
        cost_estimate=LONG,
    )(x)


def attend_grad_body(x_ref, do_ref, att_ref, lse_ref, out_ref, dk_ref, dv_ref, *, step):
    groups, _, tokens, width = x_ref.shape
    length, dim = groups * tokens, HEAD_DIM
    scale = 1.0 / dim**0.5
    fold = math.log2(math.e) * scale
    for h in range(width // dim):
        own = slice(h * dim, (h + 1) * dim)
        q = x_ref[:, 0, :, own].reshape(length, dim)
        k = x_ref[:, 1, :, own].reshape(length, dim)
        v = x_ref[:, 2, :, own].reshape(length, dim)
        kt = k.T
        for lo in range(0, length, step):
            qb = q[lo : lo + step]
            do = do_ref[lo : lo + step, own]
            p = jnp.exp2(dot_nt(k, qb) * fold - lse_ref[h, :, lo : lo + step])
            gp = dot_nt(v, do)
            do_t = do.astype(F32).T
            delta = jnp.sum(do_t * att_ref[own, lo : lo + step].astype(F32), axis=0, keepdims=True)
            gs = (p * (gp - delta)).astype(BF16)
            dv = dot(p.astype(BF16), do)
            dk = dot(gs, qb)
            if lo == 0:
                dv_ref[...] = dv
                dk_ref[...] = dk
            else:
                dv_ref[...] += dv
                dk_ref[...] += dk
            dq = (dot(kt, gs) * scale).T.astype(BF16)
            for j in range(step // tokens):
                out_ref[lo // tokens + j, 0, :, own] = dq[j * tokens : (j + 1) * tokens]
        out_ref[:, 1, :, own] = (dk_ref[...] * scale).astype(BF16).reshape(groups, tokens, dim)
        out_ref[:, 2, :, own] = dv_ref[...].astype(BF16).reshape(groups, tokens, dim)


def attend_grad(x, dout, att, lse):
    groups, _, tokens, _ = x.shape
    return pl.pallas_call(
        lambda *r: attend_grad_body(*r, step=256),
        in_specs=[VMEM] * 4,
        out_specs=VMEM,
        out_shape=jax.ShapeDtypeStruct(x.shape, BF16),
        scratch_shapes=[pltpu.VMEM((groups * tokens, HEAD_DIM), F32)] * 2,
        compiler_params=PARAMS,
        cost_estimate=FREE,
    )(x, dout, att, lse)


def chunk_rows(w_ref, y, first):
    parts = []
    for z in range(0, w_ref.shape[1], 2):
        if first:
            parts += [w_ref[y, z, :BLOCK], w_ref[y, z + 1, BLOCK // 2 :]]
        else:
            parts += [w_ref[y, z, BLOCK:], w_ref[y, z + 1, : BLOCK // 2]]
    return jnp.concatenate(parts, axis=0)


def dout_a_body(*refs):
    g_refs, w_ref, out_ref = refs[:-2], refs[-2], refs[-1]
    ys = w_ref.shape[0]
    step = g_refs[0].shape[1] // ys
    for y in range(ys):
        rows = jnp.concatenate([g[:, y * step : (y + 1) * step] for g in g_refs], axis=0)
        part = dot(rows, chunk_rows(w_ref, y, True))
        if y == 0:
            out_ref[...] = part
        else:
            out_ref[...] += part


def find_dout_a(got, w):
    return pl.pallas_call(
        dout_a_body,
        in_specs=[VMEM] * (len(got) + 1),
        out_specs=VMEM,
        out_shape=jax.ShapeDtypeStruct((sum(g.shape[0] for g in got), w.shape[3]), F32),
        compiler_params=PARAMS,
        cost_estimate=LONG,
    )(*got, w)


def dout_b_body(*refs):
    pos_ref, g_refs, w_ref, base_ref, out_ref, acc_ref = refs[0], refs[1:-4], *refs[-4:]
    tokens, cols = g_refs[0].shape
    ys = w_ref.shape[0]
    step = cols // ys
    for y in range(ys):
        rows = jnp.concatenate([g[:, y * step : (y + 1) * step] for g in g_refs], axis=0)
        part = dot(rows, chunk_rows(w_ref, y, False))
        if y == 0:
            acc_ref[...] = base_ref[...] + part
        elif y < ys - 1:
            acc_ref[...] += part
        else:
            for p in range(part.shape[0] // tokens):
                own = slice(p * tokens, (p + 1) * tokens)
                at = pl.ds(pl.multiple_of(pos_ref[p] * tokens, tokens), tokens)
                out_ref[at] = (acc_ref[own] + part[own]).astype(BF16)


def find_dout_b(pos, got, w, base):
    return pl.pallas_call(
        dout_b_body,
        in_specs=[SMEM] + [VMEM] * (len(got) + 2),
        out_specs=VMEM,
        out_shape=jax.ShapeDtypeStruct(base.shape, BF16),
        scratch_shapes=[pltpu.VMEM(base.shape, F32)],
        compiler_params=PARAMS,
        cost_estimate=FREE,
    )(pos, *got, w, base)


def own_order(pos_ref, att_ref, own_ref, tokens):
    for p in range(att_ref.shape[1] // tokens):
        at = pl.ds(pl.multiple_of(pos_ref[p] * tokens, tokens), tokens)
        own_ref[:, p * tokens : (p + 1) * tokens] = att_ref[:, at]


def term_a_body(*refs, pieces, step):
    pos_ref, g_refs, att_ref = refs[0], refs[1 : 1 + pieces], refs[1 + pieces]
    out_ref, own_ref = refs[-2:]
    ys, _, cols = out_ref.shape
    own_order(pos_ref, att_ref, own_ref, g_refs[0].shape[0])
    for y in range(ys):
        for lo in range(0, cols, step):
            at = y * cols + lo
            rows = jnp.concatenate([g[:, at : at + step] for g in g_refs], axis=0)
            out_ref[y, :, lo : lo + step] = dot(own_ref[...], rows).astype(BF16)


def find_term_a(pos, g, att, ys):
    cols = g[0].shape[1]
    width = att.shape[0]
    return pl.pallas_call(
        lambda *r: term_a_body(*r, pieces=len(g), step=512),
        in_specs=[SMEM] + [VMEM] * (len(g) + 1),
        out_specs=VMEM,
        out_shape=jax.ShapeDtypeStruct((ys, width, cols // ys), BF16),
        scratch_shapes=[pltpu.VMEM(att.shape, BF16)],
        compiler_params=PARAMS,
        cost_estimate=FREE,
    )(pos, *g, att)


def term_b_body(*refs, pieces, ways):
    pos_ref, z_ref, g_refs, att_ref = refs[0], refs[1], refs[2 : 2 + pieces], refs[2 + pieces]
    out_refs, own_ref, all_ref = refs[-2 - ways : -2], refs[-2], refs[-1]
    _, ys, rows_each, _ = all_ref.shape
    step = ways * rows_each
    own_order(pos_ref, att_ref, own_ref, g_refs[0].shape[0])
    for y in range(ys):
        rows = jnp.concatenate([g[:, y * step : (y + 1) * step] for g in g_refs], axis=0)
        flat = dot(own_ref[...], rows).T.astype(BF16)
        for z in range(ways):
            all_ref[z, y] = flat[z * rows_each : (z + 1) * rows_each]
    for d in range(ways):
        out_refs[d][...] = all_ref[lax.rem(z_ref[0] + d, ways)]


def find_term_b(pos, z_index, g, att, ys, zs):
    cols = g[0].shape[1]
    width = att.shape[0]
    piece = (ys, cols // ys // zs, width)
    return pl.pallas_call(
        lambda *r: term_b_body(*r, pieces=len(g), ways=zs),
        in_specs=[SMEM] * 2 + [VMEM] * (len(g) + 1),
        out_specs=[VMEM] * zs,
        out_shape=[jax.ShapeDtypeStruct(piece, BF16)] * zs,
        scratch_shapes=[pltpu.VMEM(att.shape, BF16), pltpu.VMEM((zs, *piece), BF16)],
        compiler_params=PARAMS,
        cost_estimate=FREE,
    )(pos, z_index, *g, att)


def total_of(values):
    total = values[0].astype(F32)
    for v in values[1:]:
        total = total + v.astype(F32)
    return total


def fold_a_body(z_ref, x_ref, *refs):
    out_refs, all_ref = refs[:-1], refs[-1]
    ways = len(out_refs)
    step = x_ref.shape[2] // ways
    for z in range(ways):
        own = slice(z * step, (z + 1) * step)
        all_ref[z] = total_of([x_ref[i, :, own] for i in range(x_ref.shape[0])]).T.astype(BF16)
    for d in range(ways):
        out_refs[d][...] = all_ref[lax.rem(z_ref[0] + d, ways)]


def fold_a(z_index, x, ways):
    _, width, cols = x.shape
    piece = (cols // ways, width)
    return pl.pallas_call(
        fold_a_body,
        in_specs=[SMEM, VMEM],
        out_specs=[VMEM] * ways,
        out_shape=[jax.ShapeDtypeStruct(piece, BF16)] * ways,
        scratch_shapes=[pltpu.VMEM((ways, *piece), BF16)],
        compiler_params=PARAMS,
        cost_estimate=LONG,
    )(z_index, x)


def fold_b_body(y_ref, *refs, count, moves):
    in_refs, out_refs, all_ref = refs[:count], refs[count:-1], refs[-1]
    ways = all_ref.shape[0]
    for y in range(ways):
        all_ref[y] = total_of([r[y] for r in in_refs])
    for ref, d in zip(out_refs, moves):
        ref[...] = all_ref[lax.rem(y_ref[0] + d, ways)].astype(ref.dtype)


def fold_b(y_index, parts, moves):
    ys, rows, width = parts[0].shape
    return pl.pallas_call(
        lambda *r: fold_b_body(*r, count=len(parts), moves=moves),
        in_specs=[SMEM] + [VMEM] * len(parts),
        out_specs=[VMEM] * len(moves),
        out_shape=[jax.ShapeDtypeStruct((rows, width), F32 if d == 0 else BF16) for d in moves],
        scratch_shapes=[pltpu.VMEM((ys, rows, width), F32)],
        compiler_params=PARAMS,
        cost_estimate=LONG,
    )(y_index, *parts)


def finish_body(odd_ref, *refs, count):
    out_ref = refs[-1]
    odd = odd_ref[0]
    for group, even_at, odd_at in ((refs[:count], 0, BLOCK // 2), (refs[count:-1], BLOCK, 0)):
        total = total_of([r[...] for r in group])
        at = pl.multiple_of(jnp.where(odd == 1, odd_at, even_at), BLOCK // 2)
        out_ref[pl.ds(at, total.shape[0])] = total


def finish(odd, first, second):
    width = first[0].shape[1]
    rows = first[0].shape[0] + second[0].shape[0]
    return pl.pallas_call(
        lambda *r: finish_body(*r, count=len(first)),
        in_specs=[SMEM] + [VMEM] * (len(first) + len(second)),
        out_specs=VMEM,
        out_shape=jax.ShapeDtypeStruct((rows, width), F32),
        compiler_params=PARAMS,
        cost_estimate=FREE,
    )(odd, *first, *second)


def solution(mesh):
    groups, spread = mesh.shape["seq"], mesh.shape["fsdp"]
    ys, zs = 4, spread // 4
    chips = groups // 2
    y_groups = [[y * zs + z for y in range(ys)] for z in range(zs)]
    z_groups = [[y * zs + z for z in range(zs)] for y in range(ys)]

    def along_x(a, d):
        return lax.ppermute(a, "seq", [(i, (i + 2 * d) % groups) for i in range(groups)])

    def swap(a):
        return lax.ppermute(a, "seq", [(i, i ^ 1) for i in range(groups)])

    def along_z(a, d):
        return lax.ppermute(a, "fsdp", [(y * zs + z, y * zs + (z + d) % zs) for y in range(ys) for z in range(zs)])

    def along_y(a, d):
        return lax.ppermute(a, "fsdp", [(y * zs + z, (y + d) % ys * zs + z) for y in range(ys) for z in range(zs)])

    def after(a, *others):
        return lax.optimization_barrier((a, *others))[0]

    def shards(queries, attn_keys, attn_values, grad_out, out_weight):
        me = lax.axis_index("seq")
        f = lax.axis_index("fsdp")
        x, core, yi, zi = me // 2, me % 2, f // zs, f % zs
        near = [(x - d) % chips * 2 for d in (0, 1, -1, 2)]
        pos = jnp.stack([n + core for n in near] + [n + 1 - core for n in near]).astype(jnp.int32)
        y_index = yi.astype(jnp.int32).reshape(1)
        z_index = zi.astype(jnp.int32).reshape(1)

        packed = pack_heads(queries, attn_keys, attn_values, groups)
        heads = lax.all_to_all(packed, "seq", 0, 0, tiled=True)
        weight = lax.all_gather(out_weight.T, "fsdp", axis=0).reshape(ys, zs, *out_weight.shape[::-1])

        chunk_a, chunk_b = pack_grad(after(grad_out, packed))
        half = chunk_a.shape[0] // 2
        left_a, right_a = along_x(chunk_a, 1), along_x(chunk_a, -1)
        att, lse = attend(heads)
        far_a = [along_x(after(left_a, att)[:half], 1), along_x(after(right_a, att)[half:], -1)]
        same_a = [chunk_a, left_a, right_a, *far_a]
        got_a = same_a + [swap(after(a, att)) for a in same_a]

        left_b, right_b = along_x(after(chunk_b, left_a), 1), along_x(after(chunk_b, right_a), -1)
        term_a = find_term_a(pos, got_a, att, ys)
        far_b = [along_x(left_b[:half], 1), along_x(right_b[half:], -1)]
        same_b = [chunk_b, left_b, right_b, *far_b]
        got_b = same_b + [swap(after(b, term_a)) for b in same_b]
        both_a = lax.all_to_all(term_a, "fsdp", 0, 0, tiled=True, axis_index_groups=y_groups)
        term_b = find_term_b(after(pos, term_a), z_index, got_b, att, ys, zs)
        part = find_dout_a(got_a, after(weight, term_a))
        dout = find_dout_b(after(pos, term_b[0]), got_b, weight, part)
        grads = attend_grad(heads, dout, att, lse)
        back = lax.all_to_all(grads, "seq", 0, 0, tiled=True)

        parts_b = [along_z(term_b[d], d) for d in (1, 7, 2, 6, 4)] + [along_z(after(term_b[d], grads), d) for d in (3, 5)]
        away_b = fold_b(y_index, [term_b[0]] + parts_b, (0, 1, 3, 2))
        sums_b = [away_b[0]] + [along_y(b, d) for b, d in zip(away_b[1:], (1, -1, 2))]
        away_a = fold_a(z_index, after(both_a, grads), zs)
        sums_a = [away_a[0]] + [along_z(away_a[d], d) for d in range(1, zs)]
        grad_q, grad_k, grad_v = unpack_heads(back)
        grad_weight = finish(z_index % 2, sums_a, sums_b).T
        return grad_q, grad_k, grad_v, grad_weight

    tokens, weights = P("fsdp", "seq", None), P("seq", "fsdp")
    return jax.shard_map(
        shards,
        mesh=mesh,
        in_specs=(tokens, tokens, tokens, tokens, weights),
        out_specs=(tokens, tokens, tokens, weights),
        check_vma=False,
    )
```

```python
import math

import jax
import jax.numpy as jnp
from jax import lax
from jax.experimental import pallas as pl
from jax.experimental.pallas import tpu as pltpu
from jax.sharding import PartitionSpec as P

HEAD_DIM = 128
BLOCK = 128
F32 = jnp.float32
BF16 = jnp.bfloat16
NT = (((1,), (1,)), ((), ()))
PARAMS = pltpu.CompilerParams(vmem_limit_bytes=24 * 1024 * 1024)
FREE = pl.CostEstimate(flops=0, transcendentals=0, bytes_accessed=0)
HUGE = pl.CostEstimate(flops=10**13, transcendentals=0, bytes_accessed=10**8)
MID = pl.CostEstimate(flops=2 * 10**10, transcendentals=0, bytes_accessed=10**6)
LONG = pl.CostEstimate(flops=10**11, transcendentals=0, bytes_accessed=10**8)
ANY = pl.BlockSpec(memory_space=pl.ANY)
VMEM = pl.BlockSpec(memory_space=pltpu.VMEM)
SMEM = pl.BlockSpec(memory_space=pltpu.SMEM)


def dot(a, b):
    return jnp.dot(a, b, preferred_element_type=F32)


def dot_nt(a, b):
    return lax.dot_general(a, b, NT, preferred_element_type=F32)


def run_copies(pairs, sems):
    copies = [pltpu.make_async_copy(src, dst, sems.at[i]) for i, (src, dst) in enumerate(pairs)]
    for c in copies:
        c.start()
    for c in copies:
        c.wait()


def pack_heads_body(q_ref, k_ref, v_ref, out_ref, sems):
    groups, _, _, width = out_ref.shape
    run_copies(
        [
            (ref.at[0, :, i * width : (i + 1) * width], out_ref.at[i, j])
            for i in range(groups)
            for j, ref in enumerate((q_ref, k_ref, v_ref))
        ],
        sems,
    )


def pack_heads(q, k, v, groups):
    tokens, width = q.shape[1], q.shape[2] // groups
    return pl.pallas_call(
        pack_heads_body,
        in_specs=[VMEM] * 3,
        out_specs=ANY,
        out_shape=jax.ShapeDtypeStruct((groups, 3, tokens, width), BF16),
        scratch_shapes=[pltpu.SemaphoreType.DMA((3 * groups,))],
        compiler_params=PARAMS,
        cost_estimate=FREE,
    )(q, k, v)


def unpack_heads_body(x_ref, q_ref, k_ref, v_ref, sems):
    groups, _, _, width = x_ref.shape
    run_copies(
        [
            (x_ref.at[i, j], ref.at[0, :, i * width : (i + 1) * width])
            for i in range(groups)
            for j, ref in enumerate((q_ref, k_ref, v_ref))
        ],
        sems,
    )


def unpack_heads(x):
    groups, _, tokens, width = x.shape
    return pl.pallas_call(
        unpack_heads_body,
        in_specs=[VMEM],
        out_specs=[ANY] * 3,
        out_shape=[jax.ShapeDtypeStruct((1, tokens, groups * width), BF16)] * 3,
        scratch_shapes=[pltpu.SemaphoreType.DMA((3 * groups,))],
        compiler_params=PARAMS,
        cost_estimate=FREE,
    )(x)


def pack_grad_body(g_ref, a_ref, b_ref, sems):
    def cols(ref, at):
        return ref.at[:, at * BLOCK : (at + 1) * BLOCK]

    pairs = []
    for t in range(g_ref.shape[2] // (3 * BLOCK)):
        pairs += [
            (cols(g_ref.at[0], 3 * t), cols(a_ref, 2 * t)),
            (cols(g_ref.at[0], 3 * t + 2), cols(a_ref, 2 * t + 1)),
            (cols(g_ref.at[0], 3 * t + 1), cols(b_ref, t)),
        ]
    run_copies(pairs, sems)


def pack_grad(g):
    tokens, width = g.shape[1:]
    return pl.pallas_call(
        pack_grad_body,
        in_specs=[VMEM],
        out_specs=[ANY] * 2,
        out_shape=[
            jax.ShapeDtypeStruct((tokens, 2 * width // 3), BF16),
            jax.ShapeDtypeStruct((tokens, width // 3), BF16),
        ],
        scratch_shapes=[pltpu.SemaphoreType.DMA((width // BLOCK,))],
        compiler_params=PARAMS,
        cost_estimate=FREE,
    )(g)


def attend_body(x_ref, att_ref, lse_ref, *, step):
    groups, _, tokens, width = x_ref.shape
    length, dim = groups * tokens, HEAD_DIM
    fold = math.log2(math.e) / dim**0.5
    for h in range(width // dim):
        own = slice(h * dim, (h + 1) * dim)
        q = x_ref[:, 0, :, own].reshape(length, dim)
        k = x_ref[:, 1, :, own].reshape(length, dim)
        vt = x_ref[:, 2, :, own].reshape(length, dim).T
        for lo in range(0, length, step):
            s = dot_nt(k, q[lo : lo + step])
            top = jnp.max(s, axis=0, keepdims=True) * fold
            e = jnp.exp2(s * fold - top)
            total = jnp.sum(e, axis=0, keepdims=True)
            att_ref[own, lo : lo + step] = (dot(vt, e.astype(BF16)) * (1.0 / total)).astype(BF16)
            lse_ref[h, :, lo : lo + step] = top + jnp.log2(total)


def attend(x):
    groups, _, tokens, width = x.shape
    heads, length = width // HEAD_DIM, groups * tokens
    return pl.pallas_call(
        lambda *r: attend_body(*r, step=256),
        in_specs=[VMEM],
        out_specs=[VMEM] * 2,
        out_shape=[
            jax.ShapeDtypeStruct((width, length), BF16),
            jax.ShapeDtypeStruct((heads, 1, length), F32),
        ],
        compiler_params=PARAMS,
        cost_estimate=LONG,
    )(x)


def attend_grad_body(x_ref, do_ref, att_ref, lse_ref, out_ref, dk_ref, dv_ref, *, step):
    groups, _, tokens, width = x_ref.shape
    length, dim = groups * tokens, HEAD_DIM
    scale = 1.0 / dim**0.5
    fold = math.log2(math.e) * scale
    for h in range(width // dim):
        own = slice(h * dim, (h + 1) * dim)
        q = x_ref[:, 0, :, own].reshape(length, dim)
        k = x_ref[:, 1, :, own].reshape(length, dim)
        v = x_ref[:, 2, :, own].reshape(length, dim)
        kt = k.T
        for lo in range(0, length, step):
            qb = q[lo : lo + step]
            do = do_ref[lo : lo + step, own]
            p = jnp.exp2(dot_nt(k, qb) * fold - lse_ref[h, :, lo : lo + step])
            gp = dot_nt(v, do)
            do_t = do.astype(F32).T
            delta = jnp.sum(do_t * att_ref[own, lo : lo + step].astype(F32), axis=0, keepdims=True)
            gs = (p * (gp - delta)).astype(BF16)
            dv = dot(p.astype(BF16), do)
            dk = dot(gs, qb)
            if lo == 0:
                dv_ref[...] = dv
                dk_ref[...] = dk
            else:
                dv_ref[...] += dv
                dk_ref[...] += dk
            dq = (dot(kt, gs) * scale).T.astype(BF16)
            for j in range(step // tokens):
                out_ref[lo // tokens + j, 0, :, own] = dq[j * tokens : (j + 1) * tokens]
        out_ref[:, 1, :, own] = (dk_ref[...] * scale).astype(BF16).reshape(groups, tokens, dim)
        out_ref[:, 2, :, own] = dv_ref[...].astype(BF16).reshape(groups, tokens, dim)


def attend_grad(x, dout, att, lse):
    groups, _, tokens, _ = x.shape
    return pl.pallas_call(
        lambda *r: attend_grad_body(*r, step=256),
        in_specs=[VMEM] * 4,
        out_specs=VMEM,
        out_shape=jax.ShapeDtypeStruct(x.shape, BF16),
        scratch_shapes=[pltpu.VMEM((groups * tokens, HEAD_DIM), F32)] * 2,
        compiler_params=PARAMS,
        cost_estimate=FREE,
    )(x, dout, att, lse)


def chunk_rows(w_ref, y, first):
    parts = []
    for z in range(0, w_ref.shape[1], 2):
        if first:
            parts += [w_ref[y, z, :BLOCK], w_ref[y, z + 1, BLOCK // 2 :]]
        else:
            parts += [w_ref[y, z, BLOCK:], w_ref[y, z + 1, : BLOCK // 2]]
    return jnp.concatenate(parts, axis=0)


def dout_a_body(*refs):
    g_refs, w_ref, out_ref = refs[:-2], refs[-2], refs[-1]
    ys = w_ref.shape[0]
    step = g_refs[0].shape[1] // ys
    for y in range(ys):
        rows = jnp.concatenate([g[:, y * step : (y + 1) * step] for g in g_refs], axis=0)
        part = dot(rows, chunk_rows(w_ref, y, True))
        if y == 0:
            out_ref[...] = part
        else:
            out_ref[...] += part


def find_dout_a(got, w):
    return pl.pallas_call(
        dout_a_body,
        in_specs=[VMEM] * (len(got) + 1),
        out_specs=VMEM,
        out_shape=jax.ShapeDtypeStruct((sum(g.shape[0] for g in got), w.shape[3]), F32),
        compiler_params=PARAMS,
        cost_estimate=LONG,
    )(*got, w)


def dout_b_body(*refs):
    pos_ref, g_refs, w_ref, base_ref, out_ref, acc_ref = refs[0], refs[1:-4], *refs[-4:]
    tokens, cols = g_refs[0].shape
    ys = w_ref.shape[0]
    step = cols // ys
    for y in range(ys):
        rows = jnp.concatenate([g[:, y * step : (y + 1) * step] for g in g_refs], axis=0)
        part = dot(rows, chunk_rows(w_ref, y, False))
        if y == 0:
            acc_ref[...] = base_ref[...] + part
        elif y < ys - 1:
            acc_ref[...] += part
        else:
            for p in range(part.shape[0] // tokens):
                own = slice(p * tokens, (p + 1) * tokens)
                at = pl.ds(pl.multiple_of(pos_ref[p] * tokens, tokens), tokens)
                out_ref[at] = (acc_ref[own] + part[own]).astype(BF16)


def find_dout_b(pos, got, w, base):
    return pl.pallas_call(
        dout_b_body,
        in_specs=[SMEM] + [VMEM] * (len(got) + 2),
        out_specs=VMEM,
        out_shape=jax.ShapeDtypeStruct(base.shape, BF16),
        scratch_shapes=[pltpu.VMEM(base.shape, F32)],
        compiler_params=PARAMS,
        cost_estimate=FREE,
    )(pos, *got, w, base)


def own_order(pos_ref, att_ref, own_ref, tokens):
    for p in range(att_ref.shape[1] // tokens):
        at = pl.ds(pl.multiple_of(pos_ref[p] * tokens, tokens), tokens)
        own_ref[:, p * tokens : (p + 1) * tokens] = att_ref[:, at]


def term_a_body(*refs, pieces, step):
    pos_ref, g_refs, att_ref = refs[0], refs[1 : 1 + pieces], refs[1 + pieces]
    out_ref, own_ref = refs[-2:]
    ys, _, cols = out_ref.shape
    own_order(pos_ref, att_ref, own_ref, g_refs[0].shape[0])
    for y in range(ys):
        for lo in range(0, cols, step):
            at = y * cols + lo
            rows = jnp.concatenate([g[:, at : at + step] for g in g_refs], axis=0)
            out_ref[y, :, lo : lo + step] = dot(own_ref[...], rows).astype(BF16)


def find_term_a(pos, g, att, ys):
    cols = g[0].shape[1]
    width = att.shape[0]
    return pl.pallas_call(
        lambda *r: term_a_body(*r, pieces=len(g), step=512),
        in_specs=[SMEM] + [VMEM] * (len(g) + 1),
        out_specs=VMEM,
        out_shape=jax.ShapeDtypeStruct((ys, width, cols // ys), BF16),
        scratch_shapes=[pltpu.VMEM(att.shape, BF16)],
        compiler_params=PARAMS,
        cost_estimate=FREE,
    )(pos, *g, att)


def term_b_body(*refs, pieces, ways):
    pos_ref, z_ref, g_refs, att_ref = refs[0], refs[1], refs[2 : 2 + pieces], refs[2 + pieces]
    out_refs, own_ref, all_ref = refs[-2 - ways : -2], refs[-2], refs[-1]
    _, ys, rows_each, _ = all_ref.shape
    step = ways * rows_each
    own_order(pos_ref, att_ref, own_ref, g_refs[0].shape[0])
    for y in range(ys):
        rows = jnp.concatenate([g[:, y * step : (y + 1) * step] for g in g_refs], axis=0)
        flat = dot(own_ref[...], rows).T.astype(BF16)
        for z in range(ways):
            all_ref[z, y] = flat[z * rows_each : (z + 1) * rows_each]
    for d in range(ways):
        out_refs[d][...] = all_ref[lax.rem(z_ref[0] + d, ways)]


def find_term_b(pos, z_index, g, att, ys, zs):
    cols = g[0].shape[1]
    width = att.shape[0]
    piece = (ys, cols // ys // zs, width)
    return pl.pallas_call(
        lambda *r: term_b_body(*r, pieces=len(g), ways=zs),
        in_specs=[SMEM] * 2 + [VMEM] * (len(g) + 1),
        out_specs=[VMEM] * zs,
        out_shape=[jax.ShapeDtypeStruct(piece, BF16)] * zs,
        scratch_shapes=[pltpu.VMEM(att.shape, BF16), pltpu.VMEM((zs, *piece), BF16)],
        compiler_params=PARAMS,
        cost_estimate=FREE,
    )(pos, z_index, *g, att)


def total_of(values):
    total = values[0].astype(F32)
    for v in values[1:]:
        total = total + v.astype(F32)
    return total


def fold_a_body(z_ref, x_ref, *refs):
    out_refs, all_ref = refs[:-1], refs[-1]
    ways = len(out_refs)
    step = x_ref.shape[2] // ways
    for z in range(ways):
        own = slice(z * step, (z + 1) * step)
        all_ref[z] = total_of([x_ref[i, :, own] for i in range(x_ref.shape[0])]).T.astype(BF16)
    for d in range(ways):
        out_refs[d][...] = all_ref[lax.rem(z_ref[0] + d, ways)]


def fold_a(z_index, x, ways):
    _, width, cols = x.shape
    piece = (cols // ways, width)
    return pl.pallas_call(
        fold_a_body,
        in_specs=[SMEM, VMEM],
        out_specs=[VMEM] * ways,
        out_shape=[jax.ShapeDtypeStruct(piece, BF16)] * ways,
        scratch_shapes=[pltpu.VMEM((ways, *piece), BF16)],
        compiler_params=PARAMS,
        cost_estimate=LONG,
    )(z_index, x)


def fold_b_body(y_ref, *refs, count, moves):
    in_refs, out_refs, all_ref = refs[:count], refs[count:-1], refs[-1]
    ways = all_ref.shape[0]
    for y in range(ways):
        all_ref[y] = total_of([r[y] for r in in_refs])
    for ref, d in zip(out_refs, moves):
        ref[...] = all_ref[lax.rem(y_ref[0] + d, ways)].astype(ref.dtype)


def fold_b(y_index, parts, moves):
    ys, rows, width = parts[0].shape
    return pl.pallas_call(
        lambda *r: fold_b_body(*r, count=len(parts), moves=moves),
        in_specs=[SMEM] + [VMEM] * len(parts),
        out_specs=[VMEM] * len(moves),
        out_shape=[jax.ShapeDtypeStruct((rows, width), F32 if d == 0 else BF16) for d in moves],
        scratch_shapes=[pltpu.VMEM((ys, rows, width), F32)],
        compiler_params=PARAMS,
        cost_estimate=LONG,
    )(y_index, *parts)


def finish_body(odd_ref, *refs, count):
    out_ref = refs[-1]
    odd = odd_ref[0]
    for group, even_at, odd_at in ((refs[:count], 0, BLOCK // 2), (refs[count:-1], BLOCK, 0)):
        total = total_of([r[...] for r in group])
        at = pl.multiple_of(jnp.where(odd == 1, odd_at, even_at), BLOCK // 2)
        out_ref[pl.ds(at, total.shape[0])] = total


def finish(odd, first, second):
    width = first[0].shape[1]
    rows = first[0].shape[0] + second[0].shape[0]
    return pl.pallas_call(
        lambda *r: finish_body(*r, count=len(first)),
        in_specs=[SMEM] + [VMEM] * (len(first) + len(second)),
        out_specs=VMEM,
        out_shape=jax.ShapeDtypeStruct((rows, width), F32),
        compiler_params=PARAMS,
        cost_estimate=FREE,
    )(odd, *first, *second)


def solution(mesh):
    groups, spread = mesh.shape["seq"], mesh.shape["fsdp"]
    ys, zs = 4, spread // 4
    chips = groups // 2
    y_groups = [[y * zs + z for y in range(ys)] for z in range(zs)]
    z_groups = [[y * zs + z for z in range(zs)] for y in range(ys)]

    def along_x(a, d):
        return lax.ppermute(a, "seq", [(i, (i + 2 * d) % groups) for i in range(groups)])

    def swap(a):
        return lax.ppermute(a, "seq", [(i, i ^ 1) for i in range(groups)])

    def along_z(a, d):
        return lax.ppermute(a, "fsdp", [(y * zs + z, y * zs + (z + d) % zs) for y in range(ys) for z in range(zs)])

    def along_y(a, d):
        return lax.ppermute(a, "fsdp", [(y * zs + z, (y + d) % ys * zs + z) for y in range(ys) for z in range(zs)])

    def after(a, *others):
        return lax.optimization_barrier((a, *others))[0]

    def shards(queries, attn_keys, attn_values, grad_out, out_weight):
        me = lax.axis_index("seq")
        f = lax.axis_index("fsdp")
        x, core, yi, zi = me // 2, me % 2, f // zs, f % zs
        near = [(x - d) % chips * 2 for d in (0, 1, -1, 2)]
        pos = jnp.stack([n + core for n in near] + [n + 1 - core for n in near]).astype(jnp.int32)
        y_index = yi.astype(jnp.int32).reshape(1)
        z_index = zi.astype(jnp.int32).reshape(1)

        packed = pack_heads(queries, attn_keys, attn_values, groups)
        heads = lax.all_to_all(packed, "seq", 0, 0, tiled=True)
        weight = lax.all_gather(out_weight.T, "fsdp", axis=0).reshape(ys, zs, *out_weight.shape[::-1])

        chunk_a, chunk_b = pack_grad(after(grad_out, packed))
        half = chunk_a.shape[0] // 2
        left_a, right_a = along_x(chunk_a, 1), along_x(chunk_a, -1)
        att, lse = attend(heads)
        far_a = [along_x(after(left_a, att)[:half], 1), along_x(after(right_a, att)[half:], -1)]
        same_a = [chunk_a, left_a, right_a, *far_a]
        got_a = same_a + [swap(after(a, att)) for a in same_a]

        left_b, right_b = along_x(after(chunk_b, left_a), 1), along_x(after(chunk_b, right_a), -1)
        term_a = find_term_a(pos, got_a, att, ys)
        far_b = [along_x(left_b[:half], 1), along_x(right_b[half:], -1)]
        same_b = [chunk_b, left_b, right_b, *far_b]
        got_b = same_b + [swap(after(b, term_a)) for b in same_b]
        both_a = lax.all_to_all(term_a, "fsdp", 0, 0, tiled=True, axis_index_groups=y_groups)
        term_b = find_term_b(after(pos, term_a), z_index, got_b, att, ys, zs)
        part = find_dout_a(got_a, after(weight, term_a))
        dout = find_dout_b(after(pos, term_b[0]), got_b, weight, part)
        grads = attend_grad(heads, dout, att, lse)
        back = lax.all_to_all(grads, "seq", 0, 0, tiled=True)

        parts_b = [along_z(term_b[d], d) for d in (1, 7, 2, 6, 4)] + [along_z(after(term_b[d], grads), d) for d in (3, 5)]
        away_b = fold_b(y_index, [term_b[0]] + parts_b, (0, 1, 3, 2))
        sums_b = [away_b[0]] + [along_y(b, d) for b, d in zip(away_b[1:], (1, -1, 2))]
        away_a = fold_a(z_index, after(both_a, grads), zs)
        sums_a = [away_a[0]] + [along_z(away_a[d], d) for d in range(1, zs)]
        grad_q, grad_k, grad_v = unpack_heads(back)
        grad_weight = finish(z_index % 2, sums_a, sums_b).T
        return grad_q, grad_k, grad_v, grad_weight

    tokens, weights = P("fsdp", "seq", None), P("seq", "fsdp")
    return jax.shard_map(
        shards,
        mesh=mesh,
        in_specs=(tokens, tokens, tokens, tokens, weights),
        out_specs=(tokens, tokens, tokens, weights),
        check_vma=False,
    )
```
